256 devices in a mesh: group: 8 (over y, x_hi), table: 32 (over z, x_lo, core).
Axes of the slice: x: 4 (x_hi: 2, x_lo: 2; x = x_hi * 2 + x_lo), y: 4, z: 8, core: 2. Of those that a mesh axis runs over, the one named last changes fastest.
Arguments:
- table_rows: float32 [8, 131072, 128], P('group', 'table'), may hold values from -6 to 6
- row_state: float32 [8, 131072], P('group', 'table'), may hold values from 0.0001 to 0.01
- parity: float32 [32, 32, 64, 128], P('table', 'group'), may hold values from -24 to 24
- parity_slot: int32 [32, 32], P('table'), may hold values from 0 to 31, each once within a row
- row_shard: int32 [8, 16384, 16, 1], P('group', 'table'), may hold values from 0 to 31; in each aligned block of 8192 rows (0 to 8191, 8192 to 16383, ..., all dimensions but the last counted through in order) at most 512 rows name the same one
- row_offset: int32 [8, 16384, 16], P('group', 'table'), may hold values from 0 to 255
- labels: int32 [16384], P('table'), may hold values 0 or 1
- first_weight: bfloat16 [16384, 1024], P('group'), may hold values from -0.046875 to 0.046875
- last_weight: float32 [1024], replicated, may hold values from -0.1875 to 0.1875
Outputs:
- updated_rows: float32 [8, 131072, 128], P('group', 'table')
- updated_state: float32 [8, 131072], P('group', 'table')
- updated_parity: float32 [32, 32, 64, 128], P('table', 'group')
- first_grad: float32 [1024, 16384], P('table', 'group')
The draws below stay inside these ranges and needn't reach their ends.
Inputs may be any that keep to these rules, and one draw needn't show every extreme that they name: `row_shard`: among the 8192 lookups of one group index and one aligned block of 512 samples, no table index is named more than 512 times, a bound that some block reaches. `parity_slot`: each row names every slot once.
All inputs are finite; a program needn't handle non-finite values. No bound on the sum of `labels` on one device may be relied on, other than what follows from the above.
Results may differ from the reference program's by a relative error of at most 0.0007.
The reference program's roundings to bfloat16 on the way (of `pooled`, `back_slope` and `pooled_grad`) count: a program that leaves them out, or rounds other values in their place, can miss the bound.
Values may be sent and summed in bfloat16 or wider, within the bound.
A program may use at most 64 MiB of HBM per device.

```python
import math
import jax
import jax.numpy as jnp
import numpy as np
from jax import lax

D = 128
H = 1024
NF_DEV = 16
B_DEV = 512
ROWS_DEV = 256
BLK = 64
BATCH = 16384
FEAT = 128
R_DEV = 4096
NS = 32
CAP = 512
N_GROUP = 8
N_TABLE = 32


def set_ends(array, rng, low, high):
    longest = array.shape.index(max(array.shape))
    spots = []
    for shift in (0, 1):
        where = [jax.random.randint(jax.random.fold_in(rng, axis), (), 0, length) for axis, length in enumerate(array.shape)]
        where[longest] = (where[longest] + shift) % array.shape[longest]
        spots.append(tuple(where))
    return array.at[spots[0]].set(low).at[spots[1]].set(high)


def block_levels(key, extent, pieces, low, top_value):
    def one(axis_at, blocks):
        steps = jax.random.uniform(jax.random.fold_in(jax.random.fold_in(key, 6), axis_at), (blocks,), jnp.float32, low / len(pieces), top_value / len(pieces))
        return jnp.repeat(jnp.exp(steps), extent[axis_at] // blocks).reshape((-1,) + (1,) * (len(extent) - axis_at - 1))

    level = one(*pieces[0])
    for cut in pieces[1:]:
        level = level * one(*cut)
    return level


def rank_table(amount, lean):
    loads = [(1 << 20) // math.isqrt(rank ** lean) + 1 for rank in range(1, amount + 1)]
    width = 1 + sum(loads) // (1 << 30)
    return np.cumsum(np.array([max(1, weight // width) for weight in loads]))


def skewed_ids(key, dims, number_of, slope):
    listing = rank_table(number_of, slope)
    lot = jax.random.randint(jax.random.fold_in(key, 1), dims, 0, int(listing[number_of - 1]))
    grade = jnp.searchsorted(jnp.asarray(listing, jnp.int32), lot, side="right")
    return jax.random.permutation(jax.random.fold_in(key, 2), number_of)[grade].astype(jnp.int32)


def deal_out(own_key, own, number, rows, amount, top, most, slope):
    sequence = jax.random.permutation(own_key, amount)
    packed, ordinary = portions_of(amount, rows * top, most, slope, True), portions_of(amount, rows * top, most, slope, False)
    places = jnp.arange(amount)

    def named(tallies, offset_by):
        used = int((tallies > 0).sum())
        fixed = max(1, used // 4)
        shifted = fixed + (places - fixed + offset_by * (used - fixed)) % max(1, amount - fixed)
        return jnp.zeros((amount,), jnp.int32).at[sequence[jnp.where(places < fixed, places, shifted)]].set(jnp.asarray(tallies, jnp.int32))

    tallies = jnp.where(number % 4 == 0, named(packed, number // 4), named(ordinary, number - number // 4 - 1))
    mixed = jax.random.permutation(jax.random.fold_in(own, 3), amount)
    giver, taker = mixed[0:amount // 2 * 2:2], mixed[1:amount // 2 * 2:2]
    margin = jnp.minimum(tallies[giver] - 1, most - tallies[taker]) // 2
    margin = jnp.where((giver == sequence[0]) | (taker == sequence[0]) | (tallies[taker] == 0), 0, jnp.maximum(margin, 0))
    shifted = jax.random.randint(jax.random.fold_in(own, 4), (amount // 2,), 0, 1 << 20) % (margin + 1)
    tallies = tallies.at[giver].add(-shifted).at[taker].add(shifted)
    items = jnp.searchsorted(jnp.cumsum(tallies), jnp.arange(rows * top), side="right").astype(jnp.int32)
    listing = items.reshape(top, rows).T
    listing = listing[jax.random.permutation(jax.random.fold_in(own, 1), rows)]
    offset_by = jax.random.randint(jax.random.fold_in(own, 2), (rows, 1), 0, top)
    return jnp.take_along_axis(listing, (jnp.arange(top)[None, :] + offset_by) % top, axis=1)


def portions_of(amount, total, bound, skew, full):
    portions = [(1 << 20) // math.isqrt(standing ** skew) + 1 for standing in range(1, amount + 1)]
    largest = bound if full else min(bound, max(-(-total // amount), total * portions[0] // sum(portions)))
    least = 1 if total - largest >= amount - 1 else 0
    given, rest = [largest] + [least] * (amount - 1), total - largest - least * (amount - 1)
    while rest > 0:
        candidates = [i for i in range(1, amount) if given[i] < largest] or [i for i in range(1, amount) if given[i] < bound]
        mass, remaining = sum([portions[i] for i in candidates]), rest
        for i in candidates:
            addition = min(bound - given[i], max(1, remaining * portions[i] // mass), rest)
            given[i] = given[i] + addition
            rest = rest - addition
    return np.array(given)


def noise(key, shape, scale, bound, pieces=(), kind=jnp.bfloat16):
    entries = scale * jax.random.normal(key, shape, jnp.float32)
    if pieces:
        entries = entries * block_levels(key, shape, pieces, -0.22, 0.18)
    return jnp.clip(entries, -bound, bound).astype(kind)


def setup_inputs(seed: int = 0) -> dict:
    key_list = jax.random.split(jax.random.key(seed), 10)
    table_rows = noise(key_list[0], (N_GROUP, N_TABLE * R_DEV, D), 1.0, 6.0, ((0, 8), (1, 32)), jnp.float32)
    row_state = jnp.clip(jnp.exp(math.log(0.01) - 4.6051702 * jax.random.uniform(key_list[1], (N_GROUP, N_TABLE * R_DEV), jnp.float32) ** block_levels(key_list[1], (N_GROUP, N_TABLE * R_DEV), ((0, 8), (1, 32)), -0.2, 0.2)), 0.0001, 0.01)
    parity = noise(key_list[2], (N_TABLE, NS, BLK, D), 4.0, 24.0, ((0, 32), (1, 8)), jnp.float32)
    parity_slot = jax.vmap(lambda own: jax.random.permutation(own, NS))(jax.random.split(key_list[3], N_TABLE)).reshape((N_TABLE, NS)).astype(jnp.int32)
    row_shard_keys = jax.random.split(jax.random.fold_in(key_list[4], 1), N_GROUP * BATCH * NF_DEV // (B_DEV * NF_DEV))
    row_shard_turns = jax.random.permutation(jax.random.fold_in(key_list[4], 3), N_GROUP * BATCH * NF_DEV // (B_DEV * NF_DEV))
    row_shard = jax.vmap(lambda own, number: deal_out(jax.random.fold_in(key_list[4], 2), own, number, B_DEV * NF_DEV, N_TABLE, 1, CAP, 1))(row_shard_keys, row_shard_turns).reshape((N_GROUP, BATCH, NF_DEV, 1))
    row_offset = set_ends(skewed_ids(key_list[5], (N_GROUP, BATCH, NF_DEV), ROWS_DEV, 2), jax.random.fold_in(key_list[5], 3), 0, ROWS_DEV - 1).astype(jnp.int32)
    labels = set_ends((jax.random.randint(key_list[6], (BATCH,), 0, 2) < 1).astype(jnp.int32), jax.random.fold_in(key_list[6], 1), 0, 1)
    first_weight = noise(key_list[7], (FEAT * D, H), (FEAT * D) ** -0.5, 0.046875, ((0, 8),))
    last_weight = noise(key_list[8], (H,), H ** -0.5, 0.1875, (), jnp.float32)
    return dict(table_rows=table_rows, row_state=row_state, parity=parity, parity_slot=parity_slot, row_shard=row_shard, row_offset=row_offset, labels=labels, first_weight=first_weight, last_weight=last_weight)


LEARN_RATE = 0.1

def silu_slope(pre_act):
    sig_pre = jax.nn.sigmoid(pre_act)
    return sig_pre * (1.0 + pre_act * (1.0 - sig_pre))

def reference(table_rows, row_state, parity, parity_slot, row_shard, row_offset, labels, first_weight, last_weight):
    feat_idx = jnp.arange(NF_DEV, dtype=jnp.int32)
    lookup_row = row_shard[..., 0] * R_DEV + feat_idx[None, None, :] * ROWS_DEV + row_offset
    gathered = jax.vmap(lambda slab_rows, where_rows: slab_rows[where_rows])(table_rows, lookup_row)
    pooled = jnp.transpose(gathered, (1, 0, 2, 3)).reshape(BATCH, FEAT * D).astype(jnp.bfloat16)
    pre_act = jnp.dot(pooled, first_weight, preferred_element_type=jnp.float32)
    activated = jax.nn.silu(pre_act)
    logits = jnp.dot(activated, last_weight, precision=lax.Precision.HIGHEST)
    residual = jax.nn.sigmoid(logits) - labels.astype(jnp.float32)
    back_slope = (residual[:, None] * last_weight[None, :] * silu_slope(pre_act)).astype(jnp.bfloat16)
    first_grad = lax.dot_general(back_slope, pooled, (((0,), (0,)), ((), ())), preferred_element_type=jnp.float32)
    pooled_grad = lax.dot_general(back_slope, first_weight, (((1,), (1,)), ((), ())), preferred_element_type=jnp.float32).astype(jnp.bfloat16)
    grad_rows = jnp.transpose(pooled_grad.reshape(BATCH, N_GROUP, NF_DEV, D), (1, 0, 2, 3)).reshape(N_GROUP, BATCH * NF_DEV, D).astype(jnp.float32)
    row_grad = jax.vmap(lambda grad_part, where_rows: jax.ops.segment_sum(grad_part, where_rows, num_segments=N_TABLE * R_DEV))(grad_rows, lookup_row.reshape(N_GROUP, BATCH * NF_DEV))
    updated_state = row_state + lax.optimization_barrier(jnp.mean(row_grad * row_grad, axis=-1))
    change = -LEARN_RATE * row_grad * lax.rsqrt(updated_state)[..., None]
    updated_rows = table_rows + change
    stripe_sum = change.reshape(N_GROUP, N_TABLE, NS, 2, BLK, D).sum(axis=(0, 3))
    table_pos = jnp.arange(N_TABLE, dtype=jnp.int32)[:, None]
    updated_parity = parity.at[table_pos, parity_slot].add(stripe_sum)
    return (updated_rows, updated_state, updated_parity, first_grad)
```

```python
import functools

import jax
import jax.numpy as jnp
from jax import lax
from jax.experimental import pallas as pl
from jax.experimental.pallas import tpu as pltpu
from jax.sharding import PartitionSpec as P

LEARN_RATE = 0.1
TABLES = 32
CAP = 512
FEATS = 16
BATCH = 512
ROWS = 4096
PER_FEATURE = 256
WIDTH = 128
HIDDEN = 1024
LANES = 128
GROUP_OF = 16
ACCS = 8
VMEM_BYTES = 56 * 2**20

f32 = jnp.float32
bf16 = jnp.bfloat16
i32 = jnp.int32


def params():
    return pltpu.CompilerParams(vmem_limit_bytes=VMEM_BYTES)


def vmem():
    return pl.BlockSpec(memory_space=pltpu.VMEM)


def smem():
    return pl.BlockSpec(memory_space=pltpu.SMEM)


def dot_nt(a, b):
    return lax.dot_general(a, b, (((1,), (1,)), ((), ())), preferred_element_type=f32)


def iota(shape, axis):
    return lax.broadcasted_iota(i32, shape, axis)


def place_kernel(target_ref, offset_ref, slot_ref, request_ref, source_ref, rank_ref):
    chunks = BATCH // LANES
    lines = chunks * FEATS
    target = jnp.concatenate([target_ref[:, c * LANES : (c + 1) * LANES] for c in range(chunks)], axis=0)
    row, col = iota((LANES, LANES), 0), iota((LANES, LANES), 1)
    before = (row < col).astype(f32).astype(bf16)
    counter = jnp.concatenate([before, jnp.ones((LANES, LANES), bf16)], axis=1)
    earlier = (iota((lines, lines), 1) < iota((lines, lines), 0)).astype(f32).astype(bf16)
    rank = jnp.zeros((lines, LANES), f32)
    for t in range(TABLES):
        named = (target == t).astype(f32)
        counts = jnp.dot(named.astype(bf16), counter, preferred_element_type=f32)
        base = jnp.dot(earlier, counts[:, LANES:].astype(bf16), preferred_element_type=f32)
        rank = rank + named * (counts[:, :LANES] + base)
    rank = rank.astype(i32)
    rank = jnp.concatenate([rank[c * FEATS : (c + 1) * FEATS] for c in range(chunks)], axis=1)
    rank_ref[...] = rank
    slot_ref[...] = target_ref[...] * CAP + rank
    owner = iota((TABLES, BATCH), 0)
    sample = iota((TABLES, BATCH), 1)
    place = iota((CAP, BATCH), 0)

    def feature(f, total):
        named = target_ref[pl.ds(f, 1), :] == owner
        first = jnp.where(named, f + 1 + 32 * (sample // 256), 0)
        second = jnp.where(named, jnp.broadcast_to(offset_ref[pl.ds(f, 1), :], named.shape), 0)
        third = jnp.where(named, sample % 256, 0)
        values = jnp.concatenate([first, second, third], axis=0).astype(f32).astype(bf16)
        chosen = (rank_ref[pl.ds(f, 1), :] == place).astype(f32).astype(bf16)
        return total + dot_nt(values, chosen)

    total = lax.fori_loop(0, FEATS, feature, jnp.zeros((3 * TABLES, CAP), f32)).astype(i32)
    first, second, third = (total[k * TABLES : (k + 1) * TABLES] for k in range(3))
    used = first > 0
    f = first % 32 - 1
    request_ref[...] = jnp.where(used, f * PER_FEATURE + second, -1)
    source_ref[...] = jnp.where(used, f * BATCH + (first // 32) * 256 + third, 0)


def place(target, offset):
    return pl.pallas_call(
        place_kernel,
        out_shape=(
            jax.ShapeDtypeStruct((FEATS, BATCH), i32),
            jax.ShapeDtypeStruct((TABLES, CAP), i32),
            jax.ShapeDtypeStruct((TABLES, CAP), i32),
        ),
        in_specs=[vmem()] * 2,
        out_specs=(vmem(),) * 3,
        scratch_shapes=[pltpu.VMEM((FEATS, BATCH), i32)],
        compiler_params=params(),
        name="place",
    )(target, offset)


def pick_rows(count, index_ref, start, table_ref, block_ref):
    def group(k, carry):
        at = pl.multiple_of(k * GROUP_OF, GROUP_OF)
        for j in range(GROUP_OF):
            block_ref[pl.ds(at + j, 1), :] = table_ref[pl.ds(index_ref[start + at + j], 1), :]
        return carry

    lax.fori_loop(0, (count + GROUP_OF - 1) // GROUP_OF, group, 0)


def serve_kernel(index_ref, count_ref, table_ref, out_ref, block_ref):
    def peer(t, carry):
        pick_rows(count_ref[t], index_ref, t * CAP, table_ref, block_ref)
        out_ref[t] = block_ref[...].astype(bf16)
        return carry

    lax.fori_loop(0, TABLES, peer, 0)


def serve(index, count, table):
    return pl.pallas_call(
        serve_kernel,
        out_shape=jax.ShapeDtypeStruct((TABLES, CAP, WIDTH), bf16),
        in_specs=[smem(), smem(), vmem()],
        out_specs=vmem(),
        scratch_shapes=[pltpu.VMEM((CAP, WIDTH), f32)],
        compiler_params=params(),
        name="serve",
    )(index, count, table)


def forward_kernel(slot_ref, returned_ref, weight_ref, pooled_ref, sum_ref, rows_ref, block_ref):
    def widen(t, carry):
        rows_ref[pl.ds(pl.multiple_of(t * CAP, CAP), CAP), :] = returned_ref[t].astype(f32)
        return carry

    lax.fori_loop(0, TABLES, widen, 0)
    for f in range(FEATS):
        pick_rows(BATCH, slot_ref, f * BATCH, rows_ref, block_ref)
        pooled_ref[:, f * WIDTH : (f + 1) * WIDTH] = block_ref[...].astype(bf16)

    def tile(m, carry):
        at = pl.ds(pl.multiple_of(m * 128, 128), 128)
        sum_ref[at, :] = jnp.dot(pooled_ref[at, :], weight_ref[...], preferred_element_type=f32)
        return carry

    lax.fori_loop(0, BATCH // 128, tile, 0)


def forward(slot, returned, weight):
    return pl.pallas_call(
        forward_kernel,
        out_shape=(
            jax.ShapeDtypeStruct((BATCH, FEATS * WIDTH), bf16),
            jax.ShapeDtypeStruct((BATCH, HIDDEN), f32),
        ),
        in_specs=[smem(), vmem(), vmem()],
        out_specs=(vmem(), vmem()),
        scratch_shapes=[pltpu.VMEM((TABLES * CAP, WIDTH), f32), pltpu.VMEM((BATCH, WIDTH), f32)],
        compiler_params=params(),
        name="forward",
    )(slot, returned, weight)


def backward_kernel(source_ref, count_ref, slope_ref, weight_ref, out_ref, rows_ref, block_ref):
    def pair(k, carry):
        at = pl.multiple_of(k * 2 * WIDTH, 2 * WIDTH)
        both = dot_nt(slope_ref[...], weight_ref[pl.ds(at, 2 * WIDTH), :]).astype(bf16).astype(f32)
        to = pl.multiple_of(k * 2 * BATCH, 2 * BATCH)
        rows_ref[pl.ds(to, BATCH), :] = both[:, :WIDTH]
        rows_ref[pl.ds(to + BATCH, BATCH), :] = both[:, WIDTH:]
        return carry

    lax.fori_loop(0, FEATS // 2, pair, 0)

    def peer(t, carry):
        pick_rows(count_ref[t], source_ref, t * CAP, rows_ref, block_ref)
        out_ref[t] = block_ref[...].astype(bf16)
        return carry

    lax.fori_loop(0, TABLES, peer, 0)


def backward(source, count, slope, weight):
    return pl.pallas_call(
        backward_kernel,
        out_shape=jax.ShapeDtypeStruct((TABLES, CAP, WIDTH), bf16),
        in_specs=[smem(), smem(), vmem(), vmem()],
        out_specs=vmem(),
        scratch_shapes=[pltpu.VMEM((FEATS * BATCH, WIDTH), f32), pltpu.VMEM((CAP, WIDTH), f32)],
        compiler_params=params(),
        name="backward",
    )(source, count, slope, weight)


def update_kernel(
    index_ref, count_ref, slot_ref, incoming_ref, table_ref, state_ref, rows_ref, new_state_ref, stripes_ref, block_ref, *accs
):
    def clear(k, carry):
        at = pl.ds(pl.multiple_of(k * 128, 128), 128)
        for acc in accs:
            acc[at, :] = jnp.zeros((128, WIDTH), f32)
        return carry

    lax.fori_loop(0, ROWS // 128, clear, 0)

    def peer(t, carry):
        block_ref[...] = incoming_ref[t].astype(f32)

        def group(k, inner):
            at = pl.multiple_of(k * ACCS, ACCS)
            for j in range(ACCS):
                row = index_ref[t * CAP + at + j]
                accs[j][pl.ds(row, 1), :] = accs[j][pl.ds(row, 1), :] + block_ref[pl.ds(at + j, 1), :]
            return inner

        return lax.fori_loop(0, (count_ref[t] + ACCS - 1) // ACCS, group, carry)

    lax.fori_loop(0, TABLES, peer, 0)
    half = WIDTH // 2
    same = iota((WIDTH, WIDTH), 0) == iota((WIDTH, WIDTH), 1)

    def stripe(s, carry):
        at = pl.ds(pl.multiple_of(s * 128, 128), 128)
        grad = accs[0][at, :]
        for acc in accs[1:]:
            grad = grad + acc[at, :]
        mean = jnp.sum(grad * grad, axis=1, keepdims=True) * (1.0 / WIDTH)
        state = jnp.sum(jnp.where(same, state_ref[pl.ds(s, 1), :], 0.0), axis=1, keepdims=True) + mean
        change = -LEARN_RATE * grad * lax.rsqrt(state)
        rows_ref[at, :] = table_ref[at, :] + change
        new_state_ref[pl.ds(s, 1), :] = jnp.sum(jnp.where(same, state, 0.0), axis=0, keepdims=True)
        stripes_ref[slot_ref[s]] = (change[:half] + change[half:]).astype(bf16)
        return carry

    lax.fori_loop(0, ROWS // 128, stripe, 0)


def update(index, count, slot, incoming, table, state):
    return pl.pallas_call(
        update_kernel,
        out_shape=(
            jax.ShapeDtypeStruct((ROWS, WIDTH), f32),
            jax.ShapeDtypeStruct((ROWS // WIDTH, WIDTH), f32),
            jax.ShapeDtypeStruct((ROWS // WIDTH, WIDTH // 2, WIDTH), bf16),
        ),
        in_specs=[smem(), smem(), smem(), vmem(), vmem(), vmem()],
        out_specs=(vmem(),) * 3,
        scratch_shapes=[pltpu.VMEM((CAP, WIDTH), f32)] + [pltpu.VMEM((ROWS + 8, WIDTH), f32)] * ACCS,
        compiler_params=params(),
        name="update",
    )(index, count, slot, incoming, table, state)


def head_slope(pre_act, label_rows, last_weight):
    activated = jax.nn.silu(pre_act)
    logits = jnp.dot(activated, last_weight, precision=lax.Precision.HIGHEST)
    residual = jax.nn.sigmoid(logits) - label_rows.astype(f32)
    sig_pre = jax.nn.sigmoid(pre_act)
    return (residual[:, None] * last_weight[None, :] * (sig_pre * (1.0 + pre_act * (1.0 - sig_pre)))).astype(bf16)


def local(
    table_rows,
    row_state,
    parity,
    parity_slot,
    row_shard,
    row_offset,
    labels,
    first_weight,
    last_weight,
):
    table = table_rows[0]
    target = jnp.transpose(row_shard[0, :, :, 0])
    offset = jnp.transpose(row_offset[0])
    slot, request, source = place(target, offset)
    sent = jnp.sum((request >= 0).astype(i32), axis=1)
    wanted = lax.all_to_all(request, "table", split_axis=0, concat_axis=0, tiled=True)
    served = jnp.sum((wanted >= 0).astype(i32), axis=1)
    rows_out = serve(jnp.maximum(wanted, 0).reshape(-1), served, table)
    returned = lax.all_to_all(rows_out, "table", split_axis=0, concat_axis=0, tiled=True)
    pooled, partial_sum = forward(slot.reshape(-1), returned, first_weight)
    share = lax.psum_scatter(partial_sum, "group", scatter_dimension=0, tiled=True)
    samples = share.shape[0]
    own = lax.dynamic_slice(labels, (lax.axis_index("group") * samples,), (samples,))
    slope = lax.all_gather(head_slope(share, own, last_weight), "group", axis=0, tiled=True)
    weight_grad = lax.dot_general(slope, pooled, (((0,), (0,)), ((), ())), preferred_element_type=f32)
    slope, weight_grad = lax.optimization_barrier((slope, weight_grad))
    first_grad = lax.psum_scatter(weight_grad, "table", scatter_dimension=0, tiled=True)
    outgoing = backward(source.reshape(-1), sent, slope, first_weight)
    incoming = lax.all_to_all(outgoing, "table", split_axis=0, concat_axis=0, tiled=True)
    segment = jnp.where(wanted >= 0, wanted, ROWS).reshape(-1)
    new_rows, new_state, stripes = update(
        segment, served, parity_slot[0], incoming, table, row_state.reshape(ROWS // WIDTH, WIDTH)
    )
    arrived = lax.psum_scatter(stripes, "group", scatter_dimension=0, tiled=True).astype(f32)
    new_parity = parity[0] + arrived
    return (new_rows[None], new_state.reshape(1, ROWS), new_parity[None], first_grad)


def solution(mesh):
    placed = (
        P("group", "table", None),
        P("group", "table"),
        P("table", "group", None, None),
        P("table", None),
        P("group", "table", None, None),
        P("group", "table", None),
        P("table"),
        P("group", None),
        P(),
    )
    return jax.shard_map(
        local,
        mesh=mesh,
        in_specs=placed,
        out_specs=(
            P("group", "table", None),
            P("group", "table"),
            P("table", "group", None, None),
            P("table", "group"),
        ),
        check_vma=False,
    )
```

```python
import functools

import jax
import jax.numpy as jnp
from jax import lax
from jax.experimental import pallas as pl
from jax.experimental.pallas import tpu as pltpu
from jax.sharding import PartitionSpec as P

LEARN_RATE = 0.1
GROUPS = 8
TABLES = 32
CAP = 512
FEATS = 16
BATCH = 512
ROWS = 4096
PER_FEATURE = 256
WIDTH = 128
HIDDEN = 1024
SHARE = BATCH // GROUPS
OWNED = 32 // GROUPS
LANES = 128
GROUP_OF = 16
ACCS = 8
VMEM_BYTES = 56 * 2**20

f32 = jnp.float32
bf16 = jnp.bfloat16
i32 = jnp.int32
MESH = pl.DeviceIdType.MESH


def params(collective_id=None):
    if collective_id is None:
        return pltpu.CompilerParams(vmem_limit_bytes=VMEM_BYTES)
    return pltpu.CompilerParams(vmem_limit_bytes=VMEM_BYTES, collective_id=collective_id, has_side_effects=True)


def vmem():
    return pl.BlockSpec(memory_space=pltpu.VMEM)


def smem():
    return pl.BlockSpec(memory_space=pltpu.SMEM)


def dot_nt(a, b):
    return lax.dot_general(a, b, (((1,), (1,)), ((), ())), preferred_element_type=f32)


def iota(shape, axis):
    return lax.broadcasted_iota(i32, shape, axis)


def place_kernel(target_ref, offset_ref, slot_ref, request_ref, source_ref, rank_ref):
    chunks = BATCH // LANES
    lines = chunks * FEATS
    target = jnp.concatenate([target_ref[:, c * LANES : (c + 1) * LANES] for c in range(chunks)], axis=0)
    row, col = iota((LANES, LANES), 0), iota((LANES, LANES), 1)
    before = (row < col).astype(f32).astype(bf16)
    counter = jnp.concatenate([before, jnp.ones((LANES, LANES), bf16)], axis=1)
    earlier = (iota((lines, lines), 1) < iota((lines, lines), 0)).astype(f32).astype(bf16)
    rank = jnp.zeros((lines, LANES), f32)
    for t in range(TABLES):
        named = (target == t).astype(f32)
        counts = jnp.dot(named.astype(bf16), counter, preferred_element_type=f32)
        base = jnp.dot(earlier, counts[:, LANES:].astype(bf16), preferred_element_type=f32)
        rank = rank + named * (counts[:, :LANES] + base)
    rank = rank.astype(i32)
    rank = jnp.concatenate([rank[c * FEATS : (c + 1) * FEATS] for c in range(chunks)], axis=1)
    rank_ref[...] = rank
    slot_ref[...] = target_ref[...] * CAP + rank
    owner = iota((TABLES, BATCH), 0)
    sample = iota((TABLES, BATCH), 1)
    place = iota((CAP, BATCH), 0)

    def feature(f, total):
        named = target_ref[pl.ds(f, 1), :] == owner
        first = jnp.where(named, f + 1 + 32 * (sample // 256), 0)
        second = jnp.where(named, jnp.broadcast_to(offset_ref[pl.ds(f, 1), :], named.shape), 0)
        third = jnp.where(named, sample % 256, 0)
        values = jnp.concatenate([first, second, third], axis=0).astype(f32).astype(bf16)
        chosen = (rank_ref[pl.ds(f, 1), :] == place).astype(f32).astype(bf16)
        return total + dot_nt(values, chosen)

    total = lax.fori_loop(0, FEATS, feature, jnp.zeros((3 * TABLES, CAP), f32)).astype(i32)
    first, second, third = (total[k * TABLES : (k + 1) * TABLES] for k in range(3))
    used = first > 0
    f = first % 32 - 1
    request_ref[...] = jnp.where(used, f * PER_FEATURE + second, -1)
    source_ref[...] = jnp.where(used, f * BATCH + (first // 32) * 256 + third, 0)


def place(target, offset):
    return pl.pallas_call(
        place_kernel,
        out_shape=(
            jax.ShapeDtypeStruct((FEATS, BATCH), i32),
            jax.ShapeDtypeStruct((TABLES, CAP), i32),
            jax.ShapeDtypeStruct((TABLES, CAP), i32),
        ),
        in_specs=[vmem()] * 2,
        out_specs=(vmem(),) * 3,
        scratch_shapes=[pltpu.VMEM((FEATS, BATCH), i32)],
        compiler_params=params(),
        name="place",
    )(target, offset)


def pick_rows(count, index_ref, start, table_ref, block_ref):
    def group(k, carry):
        at = pl.multiple_of(k * GROUP_OF, GROUP_OF)
        for j in range(GROUP_OF):
            block_ref[pl.ds(at + j, 1), :] = table_ref[pl.ds(index_ref[start + at + j], 1), :]
        return carry

    lax.fori_loop(0, (count + GROUP_OF - 1) // GROUP_OF, group, 0)


def serve_kernel(index_ref, count_ref, table_ref, out_ref, block_ref):
    def peer(t, carry):
        pick_rows(count_ref[t], index_ref, t * CAP, table_ref, block_ref)
        out_ref[t] = block_ref[...].astype(bf16)
        return carry

    lax.fori_loop(0, TABLES, peer, 0)


def serve(index, count, table):
    return pl.pallas_call(
        serve_kernel,
        out_shape=jax.ShapeDtypeStruct((TABLES, CAP, WIDTH), bf16),
        in_specs=[smem(), smem(), vmem()],
        out_specs=vmem(),
        scratch_shapes=[pltpu.VMEM((CAP, WIDTH), f32)],
        compiler_params=params(),
        name="serve",
    )(index, count, table)


def forward_kernel(slot_ref, returned_ref, weight_ref, pooled_ref, sum_ref, rows_ref, block_ref):
    def widen(t, carry):
        rows_ref[pl.ds(pl.multiple_of(t * CAP, CAP), CAP), :] = returned_ref[t].astype(f32)
        return carry

    lax.fori_loop(0, TABLES, widen, 0)
    for f in range(FEATS):
        pick_rows(BATCH, slot_ref, f * BATCH, rows_ref, block_ref)
        pooled_ref[:, f * WIDTH : (f + 1) * WIDTH] = block_ref[...].astype(bf16)

    def tile(m, carry):
        at = pl.ds(pl.multiple_of(m * 128, 128), 128)
        sum_ref[at, :] = jnp.dot(pooled_ref[at, :], weight_ref[...], preferred_element_type=f32)
        return carry

    lax.fori_loop(0, BATCH // 128, tile, 0)


def forward(slot, returned, weight):
    return pl.pallas_call(
        forward_kernel,
        out_shape=(
            jax.ShapeDtypeStruct((BATCH, FEATS * WIDTH), bf16),
            jax.ShapeDtypeStruct((BATCH, HIDDEN), f32),
        ),
        in_specs=[smem(), vmem(), vmem()],
        out_specs=(vmem(), vmem()),
        scratch_shapes=[pltpu.VMEM((TABLES * CAP, WIDTH), f32), pltpu.VMEM((BATCH, WIDTH), f32)],
        compiler_params=params(),
        name="forward",
    )(slot, returned, weight)


def backward_kernel(source_ref, count_ref, slope_ref, weight_ref, out_ref, rows_ref, block_ref):
    def pair(k, carry):
        at = pl.multiple_of(k * 2 * WIDTH, 2 * WIDTH)
        both = dot_nt(slope_ref[...], weight_ref[pl.ds(at, 2 * WIDTH), :]).astype(bf16).astype(f32)
        to = pl.multiple_of(k * 2 * BATCH, 2 * BATCH)
        rows_ref[pl.ds(to, BATCH), :] = both[:, :WIDTH]
        rows_ref[pl.ds(to + BATCH, BATCH), :] = both[:, WIDTH:]
        return carry

    lax.fori_loop(0, FEATS // 2, pair, 0)

    def peer(t, carry):
        pick_rows(count_ref[t], source_ref, t * CAP, rows_ref, block_ref)
        out_ref[t] = block_ref[...].astype(bf16)
        return carry

    lax.fori_loop(0, TABLES, peer, 0)


def backward(source, count, slope, weight):
    return pl.pallas_call(
        backward_kernel,
        out_shape=jax.ShapeDtypeStruct((TABLES, CAP, WIDTH), bf16),
        in_specs=[smem(), smem(), vmem(), vmem()],
        out_specs=vmem(),
        scratch_shapes=[pltpu.VMEM((FEATS * BATCH, WIDTH), f32), pltpu.VMEM((CAP, WIDTH), f32)],
        compiler_params=params(),
        name="backward",
    )(source, count, slope, weight)


def update_kernel(
    index_ref, count_ref, slot_ref, incoming_ref, table_ref, state_ref, rows_ref, new_state_ref, stripes_ref, block_ref, *accs
):
    def clear(k, carry):
        at = pl.ds(pl.multiple_of(k * 128, 128), 128)
        for acc in accs:
            acc[at, :] = jnp.zeros((128, WIDTH), f32)
        return carry

    lax.fori_loop(0, ROWS // 128, clear, 0)

    def peer(t, carry):
        block_ref[...] = incoming_ref[t].astype(f32)

        def group(k, inner):
            at = pl.multiple_of(k * ACCS, ACCS)
            for j in range(ACCS):
                row = index_ref[t * CAP + at + j]
                accs[j][pl.ds(row, 1), :] = accs[j][pl.ds(row, 1), :] + block_ref[pl.ds(at + j, 1), :]
            return inner

        return lax.fori_loop(0, (count_ref[t] + ACCS - 1) // ACCS, group, carry)

    lax.fori_loop(0, TABLES, peer, 0)
    half = WIDTH // 2
    same = iota((WIDTH, WIDTH), 0) == iota((WIDTH, WIDTH), 1)

    def stripe(s, carry):
        at = pl.ds(pl.multiple_of(s * 128, 128), 128)
        grad = accs[0][at, :]
        for acc in accs[1:]:
            grad = grad + acc[at, :]
        mean = jnp.sum(grad * grad, axis=1, keepdims=True) * (1.0 / WIDTH)
        state = jnp.sum(jnp.where(same, state_ref[pl.ds(s, 1), :], 0.0), axis=1, keepdims=True) + mean
        change = -LEARN_RATE * grad * lax.rsqrt(state)
        rows_ref[at, :] = table_ref[at, :] + change
        new_state_ref[pl.ds(s, 1), :] = jnp.sum(jnp.where(same, state, 0.0), axis=0, keepdims=True)
        stripes_ref[slot_ref[s]] = (change[:half] + change[half:]).astype(bf16)
        return carry

    lax.fori_loop(0, ROWS // 128, stripe, 0)


def update(index, count, slot, incoming, table, state):
    return pl.pallas_call(
        update_kernel,
        out_shape=(
            jax.ShapeDtypeStruct((ROWS, WIDTH), f32),
            jax.ShapeDtypeStruct((ROWS // WIDTH, WIDTH), f32),
            jax.ShapeDtypeStruct((ROWS // WIDTH, WIDTH // 2, WIDTH), bf16),
        ),
        in_specs=[smem(), smem(), smem(), vmem(), vmem(), vmem()],
        out_specs=(vmem(),) * 3,
        scratch_shapes=[pltpu.VMEM((CAP, WIDTH), f32)] + [pltpu.VMEM((ROWS + 8, WIDTH), f32)] * ACCS,
        compiler_params=params(),
        name="update",
    )(index, count, slot, incoming, table, state)


def greet(axis, size):
    me = lax.axis_index(axis)
    barrier = pltpu.get_barrier_semaphore()
    for d in range(1, size):
        pl.semaphore_signal(barrier, inc=1, device_id={axis: lax.rem(me + d, size)}, device_id_type=MESH)
    pl.semaphore_wait(barrier, size - 1)


def push(axis, peer, source, target, sent, got):
    return pltpu.make_async_remote_copy(
        src_ref=source, dst_ref=target, send_sem=sent, recv_sem=got, device_id={axis: peer}, device_id_type=MESH
    )


def mix_kernel(sum_ref, label_ref, last_ref, slope_ref, arrived_ref, sent, got, sent_slope, got_slope):
    me = lax.axis_index("group")
    greet("group", GROUPS)
    copies = []
    for d in range(1, GROUPS):
        peer = lax.rem(me + d, GROUPS)
        theirs = sum_ref.at[pl.ds(pl.multiple_of(peer * SHARE, SHARE), SHARE)]
        copies.append(push("group", peer, theirs, arrived_ref.at[d], sent.at[d], got.at[d]))
        copies[-1].start()
    mine = pl.ds(pl.multiple_of(me * SHARE, SHARE), SHARE)
    pre_act = sum_ref[mine, :]
    for d in range(1, GROUPS):
        copies[d - 1].wait_recv()
        pre_act = pre_act + arrived_ref[d]
    sig_pre = jax.nn.sigmoid(pre_act)
    last = last_ref[...]
    logits = jnp.sum(pre_act * sig_pre * last, axis=1, keepdims=True)
    residual = jax.nn.sigmoid(logits) - label_ref[...]
    slope_ref[mine, :] = (residual * last * (sig_pre * (1.0 + pre_act * (1.0 - sig_pre)))).astype(bf16)
    handed = []
    for d in range(1, GROUPS):
        peer = lax.rem(me + d, GROUPS)
        handed.append(push("group", peer, slope_ref.at[mine], slope_ref.at[mine], sent_slope.at[d], got_slope.at[d]))
        handed[-1].start()
    for d in range(1, GROUPS):
        copies[d - 1].wait_send()
    for d in range(1, GROUPS):
        handed[d - 1].wait_send()
        them = pl.ds(pl.multiple_of(lax.rem(me + GROUPS - d, GROUPS) * SHARE, SHARE), SHARE)
        theirs = slope_ref.at[them]
        push("group", lax.rem(me + d, GROUPS), theirs, theirs, sent_slope.at[d], got_slope.at[d]).wait_recv()


def mix(partial_sum, label, last):
    return pl.pallas_call(
        mix_kernel,
        out_shape=jax.ShapeDtypeStruct((BATCH, HIDDEN), bf16),
        in_specs=[vmem()] * 3,
        out_specs=vmem(),
        scratch_shapes=[pltpu.VMEM((GROUPS, SHARE, HIDDEN), f32)] + [pltpu.SemaphoreType.DMA((GROUPS,))] * 4,
        compiler_params=params(0),
        name="mix",
    )(partial_sum, label, last)


def stripe_kernel(stripes_ref, parity_ref, out_ref, arrived_ref, sent, got):
    me = lax.axis_index("group")
    greet("group", GROUPS)
    copies = []
    for d in range(1, GROUPS):
        peer = lax.rem(me + d, GROUPS)
        theirs = stripes_ref.at[pl.ds(peer * OWNED, OWNED)]
        copies.append(push("group", peer, theirs, arrived_ref.at[d], sent.at[d], got.at[d]))
        copies[-1].start()
    total = stripes_ref[pl.ds(me * OWNED, OWNED)].astype(f32)
    for copy in copies:
        copy.wait_recv()
    for d in range(1, GROUPS):
        total = total + arrived_ref[d].astype(f32)
    out_ref[...] = parity_ref[...] + total
    for copy in copies:
        copy.wait_send()


def stripe_sum(stripes, parity):
    return pl.pallas_call(
        stripe_kernel,
        out_shape=jax.ShapeDtypeStruct(parity.shape, f32),
        in_specs=[vmem()] * 2,
        out_specs=vmem(),
        scratch_shapes=[pltpu.VMEM((GROUPS,) + parity.shape, bf16)] + [pltpu.SemaphoreType.DMA((GROUPS,))] * 2,
        compiler_params=params(1),
        name="stripe_sum",
    )(stripes, parity)


def local(
    table_rows,
    row_state,
    parity,
    parity_slot,
    row_shard,
    row_offset,
    labels,
    first_weight,
    last_weight,
):
    table = table_rows[0]
    target = jnp.transpose(row_shard[0, :, :, 0])
    offset = jnp.transpose(row_offset[0])
    slot, request, source = place(target, offset)
    sent = jnp.sum((request >= 0).astype(i32), axis=1)
    wanted = lax.all_to_all(request, "table", split_axis=0, concat_axis=0, tiled=True)
    served = jnp.sum((wanted >= 0).astype(i32), axis=1)
    rows_out = serve(jnp.maximum(wanted, 0).reshape(-1), served, table)
    returned = lax.all_to_all(rows_out, "table", split_axis=0, concat_axis=0, tiled=True)
    pooled, partial_sum = forward(slot.reshape(-1), returned, first_weight)
    own = lax.dynamic_slice(labels, (lax.axis_index("group") * SHARE,), (SHARE,)).astype(f32)
    slope = mix(partial_sum, own[:, None], last_weight[None, :])
    weight_grad = lax.dot_general(slope, pooled, (((0,), (0,)), ((), ())), preferred_element_type=f32)
    slope, weight_grad = lax.optimization_barrier((slope, weight_grad))
    first_grad = lax.psum_scatter(weight_grad, "table", scatter_dimension=0, tiled=True)
    outgoing = backward(source.reshape(-1), sent, slope, first_weight)
    incoming = lax.all_to_all(outgoing, "table", split_axis=0, concat_axis=0, tiled=True)
    segment = jnp.where(wanted >= 0, wanted, ROWS).reshape(-1)
    new_rows, new_state, stripes = update(
        segment, served, parity_slot[0], incoming, table, row_state.reshape(ROWS // WIDTH, WIDTH)
    )
    new_parity = stripe_sum(stripes, parity[0])
    return (new_rows[None], new_state.reshape(1, ROWS), new_parity[None], first_grad)


def solution(mesh):
    placed = (
        P("group", "table", None),
        P("group", "table"),
        P("table", "group", None, None),
        P("table", None),
        P("group", "table", None, None),
        P("group", "table", None),
        P("table"),
        P("group", None),
        P(),
    )
    return jax.shard_map(
        local,
        mesh=mesh,
        in_specs=placed,
        out_specs=(
            P("group", "table", None),
            P("group", "table"),
            P("table", "group", None, None),
            P("table", "group"),
        ),
        check_vma=False,
    )
```

```python
import functools

import jax
import jax.numpy as jnp
from jax import lax
from jax.experimental import pallas as pl
from jax.experimental.pallas import tpu as pltpu
from jax.sharding import PartitionSpec as P

LEARN_RATE = 0.1
GROUPS = 8
TABLES = 32
CAP = 512
FEATS = 16
BATCH = 512
ROWS = 4096
PER_FEATURE = 256
WIDTH = 128
HIDDEN = 1024
SHARE = BATCH // GROUPS
OWNED = 32 // GROUPS
LANES = 128
GROUP_OF = 16
ACCS = 8
VMEM_BYTES = 56 * 2**20

f32 = jnp.float32
bf16 = jnp.bfloat16
i32 = jnp.int32
MESH = pl.DeviceIdType.MESH


def params(collective_id=None):
    if collective_id is None:
        return pltpu.CompilerParams(vmem_limit_bytes=VMEM_BYTES)
    return pltpu.CompilerParams(vmem_limit_bytes=VMEM_BYTES, collective_id=collective_id, has_side_effects=True)


def vmem():
    return pl.BlockSpec(memory_space=pltpu.VMEM)


def smem():
    return pl.BlockSpec(memory_space=pltpu.SMEM)


def dot_nt(a, b):
    return lax.dot_general(a, b, (((1,), (1,)), ((), ())), preferred_element_type=f32)


def iota(shape, axis):
    return lax.broadcasted_iota(i32, shape, axis)


def hail(axis, size):
    me = lax.axis_index(axis)
    barrier = pltpu.get_barrier_semaphore()
    for d in range(1, size):
        pl.semaphore_signal(barrier, inc=1, device_id={axis: lax.rem(me + d, size)}, device_id_type=MESH)


def gather_in(size):
    pl.semaphore_wait(pltpu.get_barrier_semaphore(), size - 1)


def push(axis, peer, source, target, sent, got):
    return pltpu.make_async_remote_copy(
        src_ref=source, dst_ref=target, send_sem=sent, recv_sem=got, device_id={axis: peer}, device_id_type=MESH
    )


def dma(count):
    return pltpu.SemaphoreType.DMA((count,))


def place(target_ref, offset_ref, slot_ref, source_ref, request_ref, rank_ref):
    chunks = BATCH // LANES
    lines = chunks * FEATS
    target = jnp.concatenate([target_ref[:, c * LANES : (c + 1) * LANES] for c in range(chunks)], axis=0)
    row, col = iota((LANES, LANES), 0), iota((LANES, LANES), 1)
    before = (row < col).astype(f32).astype(bf16)
    counter = jnp.concatenate([before, jnp.ones((LANES, LANES), bf16)], axis=1)
    earlier = (iota((lines, lines), 1) < iota((lines, lines), 0)).astype(f32).astype(bf16)
    rank = jnp.zeros((lines, LANES), f32)
    for t in range(TABLES):
        named = (target == t).astype(f32)
        counts = jnp.dot(named.astype(bf16), counter, preferred_element_type=f32)
        base = jnp.dot(earlier, counts[:, LANES:].astype(bf16), preferred_element_type=f32)
        rank = rank + named * (counts[:, :LANES] + base)
    rank = rank.astype(i32)
    rank = jnp.concatenate([rank[c * FEATS : (c + 1) * FEATS] for c in range(chunks)], axis=1)
    rank_ref[...] = rank
    slot_ref[...] = target_ref[...] * CAP + rank
    owner = iota((TABLES, BATCH), 0)
    sample = iota((TABLES, BATCH), 1)
    spot = iota((CAP, BATCH), 0)

    def feature(f, total):
        named = target_ref[pl.ds(f, 1), :] == owner
        first = jnp.where(named, f + 1 + 32 * (sample // 256), 0)
        second = jnp.where(named, jnp.broadcast_to(offset_ref[pl.ds(f, 1), :], named.shape), 0)
        third = jnp.where(named, sample % 256, 0)
        values = jnp.concatenate([first, second, third], axis=0).astype(f32).astype(bf16)
        chosen = (rank_ref[pl.ds(f, 1), :] == spot).astype(f32).astype(bf16)
        return total + dot_nt(values, chosen)

    total = lax.fori_loop(0, FEATS, feature, jnp.zeros((3 * TABLES, CAP), f32)).astype(i32)
    first, second, third = (total[k * TABLES : (k + 1) * TABLES] for k in range(3))
    used = first > 0
    f = first % 32 - 1
    request = jnp.where(used, f * PER_FEATURE + second, -1)
    source = jnp.where(used, f * BATCH + (first // 32) * 256 + third, 0)
    for c in range(CAP // LANES):
        request_ref[:, c, :] = request[:, c * LANES : (c + 1) * LANES]
        source_ref[:, c, :] = source[:, c * LANES : (c + 1) * LANES]


def pick(index_ref, peer, table_ref, block_ref):
    for c in range(CAP // LANES):

        def group(k, carry):
            at = pl.multiple_of(k * GROUP_OF, GROUP_OF)
            for j in range(GROUP_OF):
                row = index_ref[peer, c, at + j]
                block_ref[pl.ds(c * LANES + at + j, 1), :] = table_ref[pl.ds(row, 1), :]
            return carry

        lax.fori_loop(0, LANES // GROUP_OF, group, 0)


def trade(me, index_ref, table_ref, block_ref, rows_ref, back_ref, sent, got):
    def serve(d, carry):
        peer = lax.rem(me + d, TABLES)
        pick(index_ref, peer, table_ref, block_ref)
        rows_ref[peer] = block_ref[...].astype(bf16)
        push("table", peer, rows_ref.at[peer], back_ref.at[me], sent.at[d], got.at[d]).start()
        return carry

    lax.fori_loop(1, TABLES, serve, 0)
    pick(index_ref, me, table_ref, block_ref)
    back_ref[me] = block_ref[...].astype(bf16)
    finish(me, rows_ref, back_ref, sent, got)


def finish(me, rows_ref, back_ref, sent, got):
    def settle(d, carry):
        peer = lax.rem(me + d, TABLES)
        giver = lax.rem(me + TABLES - d, TABLES)
        push("table", peer, rows_ref.at[peer], back_ref.at[giver], sent.at[d], got.at[d]).wait()
        return carry

    lax.fori_loop(1, TABLES, settle, 0)


def fetch_kernel(
    target_ref, offset_ref, table_ref, slot_ref, source_ref, wanted_ref, back_ref,
    rank_ref, request_ref, clip_ref, index_ref, block_ref, rows_ref, copied, sent_ask, got_ask, sent, got,
):
    me = lax.axis_index("table")
    hail("table", TABLES)
    place(target_ref, offset_ref, slot_ref, source_ref, request_ref, rank_ref)
    gather_in(TABLES)

    def ask(d, carry):
        peer = lax.rem(me + d, TABLES)
        push("table", peer, request_ref.at[peer], wanted_ref.at[me], sent_ask.at[d], got_ask.at[d]).start()
        return carry

    lax.fori_loop(1, TABLES, ask, 0)
    wanted_ref[me] = request_ref[me]
    finish(me, request_ref, wanted_ref, sent_ask, got_ask)
    clip_ref[...] = jnp.clip(wanted_ref[...], 0, ROWS - 1)
    copy = pltpu.make_async_copy(clip_ref, index_ref, copied)
    copy.start()
    copy.wait()
    trade(me, index_ref, table_ref, block_ref, rows_ref, back_ref, sent, got)


def fetch(target, offset, table):
    lists = (TABLES, CAP // LANES, LANES)
    return pl.pallas_call(
        fetch_kernel,
        out_shape=(
            jax.ShapeDtypeStruct((FEATS, BATCH), i32),
            jax.ShapeDtypeStruct(lists, i32),
            jax.ShapeDtypeStruct(lists, i32),
            jax.ShapeDtypeStruct((TABLES, CAP, WIDTH), bf16),
        ),
        in_specs=[vmem()] * 3,
        out_specs=(vmem(),) * 4,
        scratch_shapes=[
            pltpu.VMEM((FEATS, BATCH), i32),
            pltpu.VMEM(lists, i32),
            pltpu.VMEM(lists, i32),
            pltpu.SMEM(lists, i32),
            pltpu.VMEM((CAP, WIDTH), f32),
            pltpu.VMEM((TABLES, CAP, WIDTH), bf16),
            pltpu.SemaphoreType.DMA,
            dma(TABLES),
            dma(TABLES),
            dma(TABLES),
            dma(TABLES),
        ],
        compiler_params=params(2),
        name="fetch",
    )(target, offset, table)


def mix_kernel(
    slot_ref, back_ref, weight_ref, label_ref, last_ref, pooled_ref, slope_ref,
    table_ref, block_ref, sum_ref, arrived_ref, sent, got, sent_slope, got_slope,
):
    me = lax.axis_index("group")
    hail("group", GROUPS)

    def widen(t, carry):
        table_ref[pl.ds(pl.multiple_of(t * CAP, CAP), CAP), :] = back_ref[t].astype(f32)
        return carry

    lax.fori_loop(0, TABLES, widen, 0)
    gather_in(GROUPS)

    def part(ref, index):
        return ref.at[pl.ds(pl.multiple_of(index * SHARE, SHARE), SHARE)]

    def pair(k, carry):
        first = lax.rem(me // 2 + 1 + k, GROUPS // 2) * 2
        base = pl.multiple_of(first * SHARE, 2 * SHARE)

        def group(b, inner):
            at = pl.multiple_of(b * 8, 8)
            for j in range(8):
                for f in range(FEATS):
                    row = slot_ref[f * BATCH + base + at + j]
                    block_ref[f, pl.ds(at + j, 1), :] = table_ref[pl.ds(row, 1), :]
            return inner

        lax.fori_loop(0, 2 * SHARE // 8, group, 0)
        pooled = jnp.concatenate([block_ref[f].astype(bf16) for f in range(FEATS)], axis=1)
        both = pl.ds(base, 2 * SHARE)
        pooled_ref[both, :] = pooled
        sum_ref[both, :] = jnp.dot(pooled, weight_ref[...], preferred_element_type=f32)
        for e in range(2):
            peer = first + e
            d = lax.rem(peer + GROUPS - me, GROUPS)

            @pl.when(d > 0)
            def _():
                push("group", peer, part(sum_ref, peer), arrived_ref.at[d], sent.at[d], got.at[d]).start()

        return carry

    lax.fori_loop(0, GROUPS // 2, pair, 0)
    mine = pl.ds(pl.multiple_of(me * SHARE, SHARE), SHARE)
    pre_act = sum_ref[mine, :]
    for d in range(1, GROUPS):
        peer = lax.rem(me + d, GROUPS)
        push("group", peer, part(sum_ref, peer), arrived_ref.at[d], sent.at[d], got.at[d]).wait()
        pre_act = pre_act + arrived_ref[d]
    sig_pre = jax.nn.sigmoid(pre_act)
    last = last_ref[...]
    logits = jnp.sum(pre_act * sig_pre * last, axis=1, keepdims=True)
    residual = jax.nn.sigmoid(logits) - label_ref[...]
    slope_ref[mine, :] = (residual * last * (sig_pre * (1.0 + pre_act * (1.0 - sig_pre)))).astype(bf16)
    for d in range(1, GROUPS):
        peer = lax.rem(me + d, GROUPS)
        push("group", peer, part(slope_ref, me), part(slope_ref, me), sent_slope.at[d], got_slope.at[d]).start()
    for d in range(1, GROUPS):
        peer = lax.rem(me + d, GROUPS)
        giver = lax.rem(me + GROUPS - d, GROUPS)
        push("group", peer, part(slope_ref, me), part(slope_ref, giver), sent_slope.at[d], got_slope.at[d]).wait()


def mix(slot, back, weight, label, last):
    return pl.pallas_call(
        mix_kernel,
        out_shape=(
            jax.ShapeDtypeStruct((BATCH, FEATS * WIDTH), bf16),
            jax.ShapeDtypeStruct((BATCH, HIDDEN), bf16),
        ),
        in_specs=[smem()] + [vmem()] * 4,
        out_specs=(vmem(), vmem()),
        scratch_shapes=[
            pltpu.VMEM((TABLES * CAP, WIDTH), f32),
            pltpu.VMEM((FEATS, 2 * SHARE, WIDTH), f32),
            pltpu.VMEM((BATCH, HIDDEN), f32),
            pltpu.VMEM((GROUPS, SHARE, HIDDEN), f32),
            dma(GROUPS),
            dma(GROUPS),
            dma(GROUPS),
            dma(GROUPS),
        ],
        compiler_params=params(0),
        name="mix",
    )(slot, back, weight, label, last)


def give_kernel(source_ref, slope_ref, weight_ref, back_ref, table_ref, block_ref, rows_ref, sent, got):
    me = lax.axis_index("table")
    hail("table", TABLES)

    def pair(k, carry):
        at = pl.multiple_of(k * 2 * WIDTH, 2 * WIDTH)
        both = dot_nt(slope_ref[...], weight_ref[pl.ds(at, 2 * WIDTH), :]).astype(bf16).astype(f32)
        to = pl.multiple_of(k * 2 * BATCH, 2 * BATCH)
        table_ref[pl.ds(to, BATCH), :] = both[:, :WIDTH]
        table_ref[pl.ds(to + BATCH, BATCH), :] = both[:, WIDTH:]
        return carry

    lax.fori_loop(0, FEATS // 2, pair, 0)
    gather_in(TABLES)
    trade(me, source_ref, table_ref, block_ref, rows_ref, back_ref, sent, got)


def give(source, slope, weight):
    return pl.pallas_call(
        give_kernel,
        out_shape=jax.ShapeDtypeStruct((TABLES, CAP, WIDTH), bf16),
        in_specs=[smem(), vmem(), vmem()],
        out_specs=vmem(),
        scratch_shapes=[
            pltpu.VMEM((FEATS * BATCH, WIDTH), f32),
            pltpu.VMEM((CAP, WIDTH), f32),
            pltpu.VMEM((TABLES, CAP, WIDTH), bf16),
            dma(TABLES),
            dma(TABLES),
        ],
        compiler_params=params(3),
        name="give",
    )(source, slope, weight)


def update_kernel(
    index_ref, count_ref, slot_ref, incoming_ref, table_ref, state_ref, rows_ref, new_state_ref, stripes_ref, block_ref, *accs
):
    def clear(k, carry):
        at = pl.ds(pl.multiple_of(k * 128, 128), 128)
        for acc in accs:
            acc[at, :] = jnp.zeros((128, WIDTH), f32)
        return carry

    lax.fori_loop(0, ROWS // 128, clear, 0)

    def peer(t, carry):
        block_ref[...] = incoming_ref[t].astype(f32)

        def group(k, inner):
            at = pl.multiple_of(k * ACCS, ACCS)
            for j in range(ACCS):
                row = index_ref[t * CAP + at + j]
                accs[j][pl.ds(row, 1), :] = accs[j][pl.ds(row, 1), :] + block_ref[pl.ds(at + j, 1), :]
            return inner

        return lax.fori_loop(0, (count_ref[t] + ACCS - 1) // ACCS, group, carry)

    lax.fori_loop(0, TABLES, peer, 0)
    half = WIDTH // 2
    same = iota((WIDTH, WIDTH), 0) == iota((WIDTH, WIDTH), 1)

    def stripe(s, carry):
        at = pl.ds(pl.multiple_of(s * 128, 128), 128)
        grad = accs[0][at, :]
        for acc in accs[1:]:
            grad = grad + acc[at, :]
        mean = jnp.sum(grad * grad, axis=1, keepdims=True) * (1.0 / WIDTH)
        state = jnp.sum(jnp.where(same, state_ref[pl.ds(s, 1), :], 0.0), axis=1, keepdims=True) + mean
        change = -LEARN_RATE * grad * lax.rsqrt(state)
        rows_ref[at, :] = table_ref[at, :] + change
        new_state_ref[pl.ds(s, 1), :] = jnp.sum(jnp.where(same, state, 0.0), axis=0, keepdims=True)
        stripes_ref[slot_ref[s]] = (change[:half] + change[half:]).astype(bf16)
        return carry

    lax.fori_loop(0, ROWS // 128, stripe, 0)


def update(index, count, slot, incoming, table, state):
    return pl.pallas_call(
        update_kernel,
        out_shape=(
            jax.ShapeDtypeStruct((ROWS, WIDTH), f32),
            jax.ShapeDtypeStruct((ROWS // WIDTH, WIDTH), f32),
            jax.ShapeDtypeStruct((ROWS // WIDTH, WIDTH // 2, WIDTH), bf16),
        ),
        in_specs=[smem(), smem(), smem(), vmem(), vmem(), vmem()],
        out_specs=(vmem(),) * 3,
        scratch_shapes=[pltpu.VMEM((CAP, WIDTH), f32)] + [pltpu.VMEM((ROWS + 8, WIDTH), f32)] * ACCS,
        compiler_params=params(),
        name="update",
    )(index, count, slot, incoming, table, state)


def stripe_kernel(stripes_ref, parity_ref, out_ref, arrived_ref, sent, got):
    me = lax.axis_index("group")
    hail("group", GROUPS)
    gather_in(GROUPS)
    copies = []
    for d in range(1, GROUPS):
        peer = lax.rem(me + d, GROUPS)
        theirs = stripes_ref.at[pl.ds(peer * OWNED, OWNED)]
        copies.append(push("group", peer, theirs, arrived_ref.at[d], sent.at[d], got.at[d]))
        copies[-1].start()
    total = stripes_ref[pl.ds(me * OWNED, OWNED)].astype(f32)
    for copy in copies:
        copy.wait_recv()
    for d in range(1, GROUPS):
        total = total + arrived_ref[d].astype(f32)
    out_ref[...] = parity_ref[...] + total
    for copy in copies:
        copy.wait_send()


def stripe_sum(stripes, parity):
    return pl.pallas_call(
        stripe_kernel,
        out_shape=jax.ShapeDtypeStruct(parity.shape, f32),
        in_specs=[vmem()] * 2,
        out_specs=vmem(),
        scratch_shapes=[pltpu.VMEM((GROUPS,) + parity.shape, bf16)] + [pltpu.SemaphoreType.DMA((GROUPS,))] * 2,
        compiler_params=params(1),
        name="stripe_sum",
    )(stripes, parity)


def local(
    table_rows,
    row_state,
    parity,
    parity_slot,
    row_shard,
    row_offset,
    labels,
    first_weight,
    last_weight,
):
    table = table_rows[0]
    target = jnp.transpose(row_shard[0, :, :, 0])
    offset = jnp.transpose(row_offset[0])
    slot, source, wanted, back = fetch(target, offset, table)
    own = lax.dynamic_slice(labels, (lax.axis_index("group") * SHARE,), (SHARE,)).astype(f32)
    pooled, slope = mix(slot.reshape(-1), back, first_weight, own[:, None], last_weight[None, :])
    weight_grad = lax.dot_general(slope, pooled, (((0,), (0,)), ((), ())), preferred_element_type=f32)
    slope, weight_grad = lax.optimization_barrier((slope, weight_grad))
    first_grad = lax.psum_scatter(weight_grad, "table", scatter_dimension=0, tiled=True)
    incoming = give(source, slope, first_weight)
    served = jnp.sum((wanted >= 0).astype(i32), axis=(1, 2))
    segment = jnp.where(wanted >= 0, wanted, ROWS).reshape(-1)
    new_rows, new_state, stripes = update(
        segment, served, parity_slot[0], incoming, table, row_state.reshape(ROWS // WIDTH, WIDTH)
    )
    new_parity = stripe_sum(stripes, parity[0])
    return (new_rows[None], new_state.reshape(1, ROWS), new_parity[None], first_grad)


def solution(mesh):
    placed = (
        P("group", "table", None),
        P("group", "table"),
        P("table", "group", None, None),
        P("table", None),
        P("group", "table", None, None),
        P("group", "table", None),
        P("table"),
        P("group", None),
        P(),
    )
    return jax.shard_map(
        local,
        mesh=mesh,
        in_specs=placed,
        out_specs=(
            P("group", "table", None),
            P("group", "table"),
            P("table", "group", None, None),
            P("table", "group"),
        ),
        check_vma=False,
    )
```

```python
import functools

import jax
import jax.numpy as jnp
from jax import lax
from jax.experimental import pallas as pl
from jax.experimental.pallas import tpu as pltpu
from jax.sharding import PartitionSpec as P

LEARN_RATE = 0.1
GROUPS = 8
TABLES = 32
CAP = 512
FEATS = 16
BATCH = 512
ROWS = 4096
PER_FEATURE = 256
WIDTH = 128
HIDDEN = 1024
NEAR = 4
PLANES = TABLES // NEAR
OUT_ROWS = HIDDEN // TABLES
EARLY = 9
SHARE = BATCH // GROUPS
OWNED = 32 // GROUPS
LANES = 128
GROUP_OF = 16
ACCS = 8
VMEM_BYTES = 56 * 2**20

f32 = jnp.float32
bf16 = jnp.bfloat16
i32 = jnp.int32
MESH = pl.DeviceIdType.MESH


def params(collective_id=None):
    if collective_id is None:
        return pltpu.CompilerParams(vmem_limit_bytes=VMEM_BYTES)
    return pltpu.CompilerParams(vmem_limit_bytes=VMEM_BYTES, collective_id=collective_id, has_side_effects=True)


def vmem():
    return pl.BlockSpec(memory_space=pltpu.VMEM)


def smem():
    return pl.BlockSpec(memory_space=pltpu.SMEM)


def dot_nt(a, b):
    return lax.dot_general(a, b, (((1,), (1,)), ((), ())), preferred_element_type=f32)


def iota(shape, axis):
    return lax.broadcasted_iota(i32, shape, axis)


def hail(axis, size):
    me = lax.axis_index(axis)
    barrier = pltpu.get_barrier_semaphore()
    for d in range(1, size):
        pl.semaphore_signal(barrier, inc=1, device_id={axis: lax.rem(me + d, size)}, device_id_type=MESH)


def gather_in(size):
    pl.semaphore_wait(pltpu.get_barrier_semaphore(), size - 1)


def push(axis, peer, source, target, sent, got):
    return pltpu.make_async_remote_copy(
        src_ref=source, dst_ref=target, send_sem=sent, recv_sem=got, device_id={axis: peer}, device_id_type=MESH
    )


def dma(count):
    return pltpu.SemaphoreType.DMA((count,))


def place(target_ref, offset_ref, slot_ref, source_ref, request_ref, rank_ref):
    chunks = BATCH // LANES
    lines = chunks * FEATS
    target = jnp.concatenate([target_ref[:, c * LANES : (c + 1) * LANES] for c in range(chunks)], axis=0)
    row, col = iota((LANES, LANES), 0), iota((LANES, LANES), 1)
    before = (row < col).astype(f32).astype(bf16)
    counter = jnp.concatenate([before, jnp.ones((LANES, LANES), bf16)], axis=1)
    earlier = (iota((lines, lines), 1) < iota((lines, lines), 0)).astype(f32).astype(bf16)
    rank = jnp.zeros((lines, LANES), f32)
    for t in range(TABLES):
        named = (target == t).astype(f32)
        counts = jnp.dot(named.astype(bf16), counter, preferred_element_type=f32)
        base = jnp.dot(earlier, counts[:, LANES:].astype(bf16), preferred_element_type=f32)
        rank = rank + named * (counts[:, :LANES] + base)
    rank = rank.astype(i32)
    rank = jnp.concatenate([rank[c * FEATS : (c + 1) * FEATS] for c in range(chunks)], axis=1)
    rank_ref[...] = rank
    slot_ref[...] = target_ref[...] * CAP + rank
    owner = iota((TABLES, BATCH), 0)
    sample = iota((TABLES, BATCH), 1)
    spot = iota((CAP, BATCH), 0)

    def feature(f, total):
        named = target_ref[pl.ds(f, 1), :] == owner
        first = jnp.where(named, f + 1 + 32 * (sample // 256), 0)
        second = jnp.where(named, jnp.broadcast_to(offset_ref[pl.ds(f, 1), :], named.shape), 0)
        third = jnp.where(named, sample % 256, 0)
        values = jnp.concatenate([first, second, third], axis=0).astype(f32).astype(bf16)
        chosen = (rank_ref[pl.ds(f, 1), :] == spot).astype(f32).astype(bf16)
        return total + dot_nt(values, chosen)

    total = lax.fori_loop(0, FEATS, feature, jnp.zeros((3 * TABLES, CAP), f32)).astype(i32)
    first, second, third = (total[k * TABLES : (k + 1) * TABLES] for k in range(3))
    used = first > 0
    f = first % 32 - 1
    request = jnp.where(used, f * PER_FEATURE + second, -1)
    source = jnp.where(used, f * BATCH + (first // 32) * 256 + third, 0)
    for c in range(CAP // LANES):
        request_ref[:, c, :] = request[:, c * LANES : (c + 1) * LANES]
        source_ref[:, c, :] = source[:, c * LANES : (c + 1) * LANES]


def pick(index_ref, peer, table_ref, block_ref):
    for c in range(CAP // LANES):

        def group(k, carry):
            at = pl.multiple_of(k * GROUP_OF, GROUP_OF)
            for j in range(GROUP_OF):
                row = index_ref[peer, c, at + j]
                block_ref[pl.ds(c * LANES + at + j, 1), :] = table_ref[pl.ds(row, 1), :]
            return carry

        lax.fori_loop(0, LANES // GROUP_OF, group, 0)


def trade(me, first, last, index_ref, table_ref, block_ref, rows_ref, back_ref, sent, got):
    def serve(d, carry):
        peer, _ = route(me, d)
        pick(index_ref, peer, table_ref, block_ref)
        rows_ref[peer] = block_ref[...].astype(bf16)
        push("table", peer, rows_ref.at[peer], back_ref.at[me], sent.at[d], got.at[d]).start()
        return carry

    lax.fori_loop(first, last, serve, 0)
    if last == TABLES:
        pick(index_ref, me, table_ref, block_ref)
        back_ref[me] = block_ref[...].astype(bf16)


def route(me, k):
    z, q = me // NEAR, lax.rem(me, NEAR)
    turn, step = lax.rem(k, PLANES), k // PLANES
    by = (turn + 1) // 2 * (2 * lax.rem(turn, 2) - 1)
    peer = lax.rem(z + by + PLANES, PLANES) * NEAR + lax.rem(q + step, NEAR)
    giver = lax.rem(z - by + PLANES, PLANES) * NEAR + lax.rem(q - step + NEAR, NEAR)
    return peer, giver


def finish(me, rows_ref, back_ref, sent, got):
    def settle(d, carry):
        peer, giver = route(me, d)
        push("table", peer, rows_ref.at[peer], back_ref.at[giver], sent.at[d], got.at[d]).wait()
        return carry

    lax.fori_loop(1, TABLES, settle, 0)


def fetch_kernel(
    target_ref, offset_ref, table_ref, slot_ref, source_ref, wanted_ref, back_ref,
    rank_ref, request_ref, clip_ref, index_ref, block_ref, rows_ref, copied, sent_ask, got_ask, sent, got,
):
    me = lax.axis_index("table")
    hail("table", TABLES)
    place(target_ref, offset_ref, slot_ref, source_ref, request_ref, rank_ref)
    gather_in(TABLES)

    def ask(d, carry):
        peer, _ = route(me, d)
        push("table", peer, request_ref.at[peer], wanted_ref.at[me], sent_ask.at[d], got_ask.at[d]).start()
        return carry

    lax.fori_loop(1, TABLES, ask, 0)
    wanted_ref[me] = request_ref[me]
    finish(me, request_ref, wanted_ref, sent_ask, got_ask)
    clip_ref[...] = jnp.clip(wanted_ref[...], 0, ROWS - 1)
    copy = pltpu.make_async_copy(clip_ref, index_ref, copied)
    copy.start()
    copy.wait()
    trade(me, 1, TABLES, index_ref, table_ref, block_ref, rows_ref, back_ref, sent, got)
    finish(me, rows_ref, back_ref, sent, got)


def fetch(target, offset, table):
    lists = (TABLES, CAP // LANES, LANES)
    return pl.pallas_call(
        fetch_kernel,
        out_shape=(
            jax.ShapeDtypeStruct((FEATS, BATCH), i32),
            jax.ShapeDtypeStruct(lists, i32),
            jax.ShapeDtypeStruct(lists, i32),
            jax.ShapeDtypeStruct((TABLES, CAP, WIDTH), bf16),
        ),
        in_specs=[vmem()] * 3,
        out_specs=(vmem(),) * 4,
        scratch_shapes=[
            pltpu.VMEM((FEATS, BATCH), i32),
            pltpu.VMEM(lists, i32),
            pltpu.VMEM(lists, i32),
            pltpu.SMEM(lists, i32),
            pltpu.VMEM((CAP, WIDTH), f32),
            pltpu.VMEM((TABLES, CAP, WIDTH), bf16),
            pltpu.SemaphoreType.DMA,
            dma(TABLES),
            dma(TABLES),
            dma(TABLES),
            dma(TABLES),
        ],
        compiler_params=params(2),
        name="fetch",
    )(target, offset, table)


def mix_kernel(
    slot_ref, back_ref, weight_ref, label_ref, last_ref, pooled_ref, slope_ref,
    table_ref, block_ref, sum_ref, arrived_ref, sent, got, sent_slope, got_slope,
):
    me = lax.axis_index("group")
    hail("group", GROUPS)

    def widen(t, carry):
        table_ref[pl.ds(pl.multiple_of(t * CAP, CAP), CAP), :] = back_ref[t].astype(f32)
        return carry

    lax.fori_loop(0, TABLES, widen, 0)
    gather_in(GROUPS)

    def part(ref, index):
        return ref.at[pl.ds(pl.multiple_of(index * SHARE, SHARE), SHARE)]

    def pair(k, carry):
        first = lax.rem(me // 2 + 1 + k, GROUPS // 2) * 2
        base = pl.multiple_of(first * SHARE, 2 * SHARE)

        def group(b, inner):
            at = pl.multiple_of(b * 8, 8)
            for j in range(8):
                for f in range(FEATS):
                    row = slot_ref[f * BATCH + base + at + j]
                    block_ref[f, pl.ds(at + j, 1), :] = table_ref[pl.ds(row, 1), :]
            return inner

        lax.fori_loop(0, 2 * SHARE // 8, group, 0)
        pooled = jnp.concatenate([block_ref[f].astype(bf16) for f in range(FEATS)], axis=1)
        both = pl.ds(base, 2 * SHARE)
        pooled_ref[both, :] = pooled
        sum_ref[both, :] = jnp.dot(pooled, weight_ref[...], preferred_element_type=f32)
        for e in range(2):
            peer = first + e
            d = lax.rem(peer + GROUPS - me, GROUPS)

            @pl.when(d > 0)
            def _():
                push("group", peer, part(sum_ref, peer), arrived_ref.at[d], sent.at[d], got.at[d]).start()

        return carry

    lax.fori_loop(0, GROUPS // 2, pair, 0)
    mine = pl.ds(pl.multiple_of(me * SHARE, SHARE), SHARE)
    pre_act = sum_ref[mine, :]
    for d in range(1, GROUPS):
        peer = lax.rem(me + d, GROUPS)
        push("group", peer, part(sum_ref, peer), arrived_ref.at[d], sent.at[d], got.at[d]).wait()
        pre_act = pre_act + arrived_ref[d]
    sig_pre = jax.nn.sigmoid(pre_act)
    last = last_ref[...]
    logits = jnp.sum(pre_act * sig_pre * last, axis=1, keepdims=True)
    residual = jax.nn.sigmoid(logits) - label_ref[...]
    slope_ref[mine, :] = (residual * last * (sig_pre * (1.0 + pre_act * (1.0 - sig_pre)))).astype(bf16)
    for d in range(1, GROUPS):
        peer = lax.rem(me + d, GROUPS)
        push("group", peer, part(slope_ref, me), part(slope_ref, me), sent_slope.at[d], got_slope.at[d]).start()
    for d in range(1, GROUPS):
        peer = lax.rem(me + d, GROUPS)
        giver = lax.rem(me + GROUPS - d, GROUPS)
        push("group", peer, part(slope_ref, me), part(slope_ref, giver), sent_slope.at[d], got_slope.at[d]).wait()


def mix(slot, back, weight, label, last):
    return pl.pallas_call(
        mix_kernel,
        out_shape=(
            jax.ShapeDtypeStruct((BATCH, FEATS * WIDTH), bf16),
            jax.ShapeDtypeStruct((BATCH, HIDDEN), bf16),
        ),
        in_specs=[smem()] + [vmem()] * 4,
        out_specs=(vmem(), vmem()),
        scratch_shapes=[
            pltpu.VMEM((TABLES * CAP, WIDTH), f32),
            pltpu.VMEM((FEATS, 2 * SHARE, WIDTH), f32),
            pltpu.VMEM((BATCH, HIDDEN), f32),
            pltpu.VMEM((GROUPS, SHARE, HIDDEN), f32),
            dma(GROUPS),
            dma(GROUPS),
            dma(GROUPS),
            dma(GROUPS),
        ],
        compiler_params=params(0),
        name="mix",
    )(slot, back, weight, label, last)


def give_kernel(
    source_ref, slope_ref, pooled_ref, weight_ref, back_ref, packed_ref,
    table_ref, block_ref, rows_ref, grad_ref, near_ref, across_ref, sent, got, sent_near, got_near, sent_across, got_across,
):
    me = lax.axis_index("table")
    core, side = lax.rem(me, 2), lax.rem(me // 2, 2)
    other, across = me + 1 - 2 * core, me + 2 - 4 * side
    hail("table", TABLES)

    def pair(k, carry):
        at = pl.multiple_of(k * 2 * WIDTH, 2 * WIDTH)
        both = dot_nt(slope_ref[...], weight_ref[pl.ds(at, 2 * WIDTH), :]).astype(bf16).astype(f32)
        to = pl.multiple_of(k * 2 * BATCH, 2 * BATCH)
        table_ref[pl.ds(to, BATCH), :] = both[:, :WIDTH]
        table_ref[pl.ds(to + BATCH, BATCH), :] = both[:, WIDTH:]
        return carry

    lax.fori_loop(0, FEATS // 2, pair, 0)
    gather_in(TABLES)
    trade(me, 1, EARLY, source_ref, table_ref, block_ref, rows_ref, back_ref, sent, got)

    def to_near(z):
        return push("table", other, grad_ref.at[z, :, 1 - core], near_ref.at[z], sent_near.at[z], got_near.at[z])

    def to_across(z):
        return push("table", across, grad_ref.at[z, 1 - side, core], across_ref.at[z], sent_across.at[z], got_across.at[z])

    def outer(z, carry):
        at = pl.multiple_of(z * LANES, LANES)
        part = lax.dot_general(
            slope_ref[:, pl.ds(at, LANES)], pooled_ref[...], (((0,), (0,)), ((), ())), preferred_element_type=f32
        )
        grad_ref[z] = part.reshape(grad_ref.shape[1:])
        to_near(z).start()
        return carry

    lax.fori_loop(0, PLANES, outer, 0)
    trade(me, EARLY, TABLES, source_ref, table_ref, block_ref, rows_ref, back_ref, sent, got)

    def fold(z, carry):
        to_near(z).wait()
        for x in range(2):
            grad_ref[z, x, core] = grad_ref[z, x, core] + near_ref[z, x]
        to_across(z).start()
        return carry

    lax.fori_loop(0, PLANES, fold, 0)

    def seal(z, carry):
        to_across(z).wait()
        total = grad_ref[z, side, core] + across_ref[z]
        top = jnp.max(jnp.abs(total), axis=1, keepdims=True)
        power = jnp.ceil(jnp.log2(jnp.clip(top * 1.0001, 1e-30, 1e30))) - 15.0
        scaled = jnp.floor(total * jnp.exp2(-power) + 0.5).astype(i32)
        k = lax.rem(z - me // NEAR + PLANES, PLANES)
        packed_ref[k, :, : FEATS * WIDTH] = scaled.astype(jnp.int16)
        packed_ref[k, :, FEATS * WIDTH :] = jnp.broadcast_to(power.astype(i32), (OUT_ROWS, LANES)).astype(jnp.int16)
        return carry

    lax.fori_loop(0, PLANES, seal, 0)
    finish(me, rows_ref, back_ref, sent, got)


def give(source, slope, pooled, weight):
    piece = (OUT_ROWS, FEATS * WIDTH)
    return pl.pallas_call(
        give_kernel,
        out_shape=(
            jax.ShapeDtypeStruct((TABLES, CAP, WIDTH), bf16),
            jax.ShapeDtypeStruct((PLANES, OUT_ROWS, FEATS * WIDTH + LANES), jnp.int16),
        ),
        in_specs=[smem(), vmem(), vmem(), vmem()],
        out_specs=(vmem(), vmem()),
        scratch_shapes=[
            pltpu.VMEM((FEATS * BATCH, WIDTH), f32),
            pltpu.VMEM((CAP, WIDTH), f32),
            pltpu.VMEM((TABLES, CAP, WIDTH), bf16),
            pltpu.VMEM((PLANES, 2, 2) + piece, f32),
            pltpu.VMEM((PLANES, 2) + piece, f32),
            pltpu.VMEM((PLANES,) + piece, f32),
            dma(TABLES),
            dma(TABLES),
            dma(PLANES),
            dma(PLANES),
            dma(PLANES),
            dma(PLANES),
        ],
        compiler_params=params(3),
        name="give",
    )(source, slope, pooled, weight)


def unpack(packed):
    power = packed[:, FEATS * WIDTH : FEATS * WIDTH + 1].astype(f32)
    return packed[:, : FEATS * WIDTH].astype(f32) * jnp.exp2(power)


def sum_planes(packed):
    total = unpack(packed[0])
    for k in range(1, PLANES):
        ring = [(t, (t + NEAR * k) % TABLES) for t in range(TABLES)]
        total = total + unpack(lax.ppermute(packed[k], "table", ring))
    return total


def update_kernel(
    index_ref, count_ref, slot_ref, incoming_ref, table_ref, state_ref, rows_ref, new_state_ref, stripes_ref, block_ref, *accs
):
    def clear(k, carry):
        at = pl.ds(pl.multiple_of(k * 128, 128), 128)
        for acc in accs:
            acc[at, :] = jnp.zeros((128, WIDTH), f32)
        return carry

    lax.fori_loop(0, ROWS // 128, clear, 0)

    def peer(t, carry):
        block_ref[...] = incoming_ref[t].astype(f32)

        def group(k, inner):
            at = pl.multiple_of(k * ACCS, ACCS)
            for j in range(ACCS):
                row = index_ref[t * CAP + at + j]
                accs[j][pl.ds(row, 1), :] = accs[j][pl.ds(row, 1), :] + block_ref[pl.ds(at + j, 1), :]
            return inner

        return lax.fori_loop(0, (count_ref[t] + ACCS - 1) // ACCS, group, carry)

    lax.fori_loop(0, TABLES, peer, 0)
    half = WIDTH // 2
    same = iota((WIDTH, WIDTH), 0) == iota((WIDTH, WIDTH), 1)

    def stripe(s, carry):
        at = pl.ds(pl.multiple_of(s * 128, 128), 128)
        grad = accs[0][at, :]
        for acc in accs[1:]:
            grad = grad + acc[at, :]
        mean = jnp.sum(grad * grad, axis=1, keepdims=True) * (1.0 / WIDTH)
        state = jnp.sum(jnp.where(same, state_ref[pl.ds(s, 1), :], 0.0), axis=1, keepdims=True) + mean
        change = -LEARN_RATE * grad * lax.rsqrt(state)
        rows_ref[at, :] = table_ref[at, :] + change
        new_state_ref[pl.ds(s, 1), :] = jnp.sum(jnp.where(same, state, 0.0), axis=0, keepdims=True)
        stripes_ref[slot_ref[s]] = (change[:half] + change[half:]).astype(bf16)
        return carry

    lax.fori_loop(0, ROWS // 128, stripe, 0)


def update(index, count, slot, incoming, table, state):
    return pl.pallas_call(
        update_kernel,
        out_shape=(
            jax.ShapeDtypeStruct((ROWS, WIDTH), f32),
            jax.ShapeDtypeStruct((ROWS // WIDTH, WIDTH), f32),
            jax.ShapeDtypeStruct((ROWS // WIDTH, WIDTH // 2, WIDTH), bf16),
        ),
        in_specs=[smem(), smem(), smem(), vmem(), vmem(), vmem()],
        out_specs=(vmem(),) * 3,
        scratch_shapes=[pltpu.VMEM((CAP, WIDTH), f32)] + [pltpu.VMEM((ROWS + 8, WIDTH), f32)] * ACCS,
        compiler_params=params(),
        name="update",
    )(index, count, slot, incoming, table, state)


def stripe_kernel(stripes_ref, parity_ref, out_ref, arrived_ref, sent, got):
    me = lax.axis_index("group")
    hail("group", GROUPS)
    gather_in(GROUPS)
    copies = []
    for d in range(1, GROUPS):
        peer = lax.rem(me + d, GROUPS)
        theirs = stripes_ref.at[pl.ds(peer * OWNED, OWNED)]
        copies.append(push("group", peer, theirs, arrived_ref.at[d], sent.at[d], got.at[d]))
        copies[-1].start()
    total = stripes_ref[pl.ds(me * OWNED, OWNED)].astype(f32)
    for copy in copies:
        copy.wait_recv()
    for d in range(1, GROUPS):
        total = total + arrived_ref[d].astype(f32)
    out_ref[...] = parity_ref[...] + total
    for copy in copies:
        copy.wait_send()


def stripe_sum(stripes, parity):
    return pl.pallas_call(
        stripe_kernel,
        out_shape=jax.ShapeDtypeStruct(parity.shape, f32),
        in_specs=[vmem()] * 2,
        out_specs=vmem(),
        scratch_shapes=[pltpu.VMEM((GROUPS,) + parity.shape, bf16)] + [pltpu.SemaphoreType.DMA((GROUPS,))] * 2,
        compiler_params=params(1),
        name="stripe_sum",
    )(stripes, parity)


def local(
    table_rows,
    row_state,
    parity,
    parity_slot,
    row_shard,
    row_offset,
    labels,
    first_weight,
    last_weight,
):
    table = table_rows[0]
    target = jnp.transpose(row_shard[0, :, :, 0])
    offset = jnp.transpose(row_offset[0])
    slot, source, wanted, back = fetch(target, offset, table)
    own = lax.dynamic_slice(labels, (lax.axis_index("group") * SHARE,), (SHARE,)).astype(f32)
    pooled, slope = mix(slot.reshape(-1), back, first_weight, own[:, None], last_weight[None, :])
    incoming, packed = give(source, slope, pooled, first_weight)
    first_grad = sum_planes(packed)
    served = jnp.sum((wanted >= 0).astype(i32), axis=(1, 2))
    segment = jnp.where(wanted >= 0, wanted, ROWS).reshape(-1)
    new_rows, new_state, stripes = update(
        segment, served, parity_slot[0], incoming, table, row_state.reshape(ROWS // WIDTH, WIDTH)
    )
    new_parity = stripe_sum(stripes, parity[0])
    return (new_rows[None], new_state.reshape(1, ROWS), new_parity[None], first_grad)


def solution(mesh):
    placed = (
        P("group", "table", None),
        P("group", "table"),
        P("table", "group", None, None),
        P("table", None),
        P("group", "table", None, None),
        P("group", "table", None),
        P("table"),
        P("group", None),
        P(),
    )
    return jax.shard_map(
        local,
        mesh=mesh,
        in_specs=placed,
        out_specs=(
            P("group", "table", None),
            P("group", "table"),
            P("table", "group", None, None),
            P("table", "group"),
        ),
        check_vma=False,
    )
```

```python
import functools

import jax
import jax.numpy as jnp
from jax import lax
from jax.experimental import pallas as pl
from jax.experimental.pallas import tpu as pltpu
from jax.sharding import PartitionSpec as P

LEARN_RATE = 0.1
GROUPS = 8
TABLES = 32
CAP = 512
FEATS = 16
BATCH = 512
ROWS = 4096
PER_FEATURE = 256
WIDTH = 128
HIDDEN = 1024
NEAR = 4
PLANES = TABLES // NEAR
OUT_ROWS = HIDDEN // TABLES
EARLY = 9
SHARE = BATCH // GROUPS
OWNED = 32 // GROUPS
LANES = 128
GROUP_OF = 16
ACCS = 8
VMEM_BYTES = 56 * 2**20

f32 = jnp.float32
bf16 = jnp.bfloat16
i32 = jnp.int32
MESH = pl.DeviceIdType.MESH


def params(collective_id=None):
    if collective_id is None:
        return pltpu.CompilerParams(vmem_limit_bytes=VMEM_BYTES)
    return pltpu.CompilerParams(vmem_limit_bytes=VMEM_BYTES, collective_id=collective_id, has_side_effects=True)


def vmem():
    return pl.BlockSpec(memory_space=pltpu.VMEM)


def smem():
    return pl.BlockSpec(memory_space=pltpu.SMEM)


def dot_nt(a, b):
    return lax.dot_general(a, b, (((1,), (1,)), ((), ())), preferred_element_type=f32)


def iota(shape, axis):
    return lax.broadcasted_iota(i32, shape, axis)


def hail(axis, size):
    me = lax.axis_index(axis)
    barrier = pltpu.get_barrier_semaphore()
    for d in range(1, size):
        pl.semaphore_signal(barrier, inc=1, device_id={axis: lax.rem(me + d, size)}, device_id_type=MESH)


def gather_in(size):
    pl.semaphore_wait(pltpu.get_barrier_semaphore(), size - 1)


def push(axis, peer, source, target, sent, got):
    return pltpu.make_async_remote_copy(
        src_ref=source, dst_ref=target, send_sem=sent, recv_sem=got, device_id={axis: peer}, device_id_type=MESH
    )


def dma(count):
    return pltpu.SemaphoreType.DMA((count,))


def place(target_ref, offset_ref, slot_ref, source_ref, request_ref, rank_ref):
    chunks = BATCH // LANES
    lines = chunks * FEATS
    target = target_ref[...]
    row, col = iota((LANES, LANES), 0), iota((LANES, LANES), 1)
    before = (row < col).astype(f32).astype(bf16)
    counter = jnp.concatenate([before, jnp.ones((LANES, LANES), bf16)], axis=1)
    earlier = (iota((lines, lines), 1) < iota((lines, lines), 0)).astype(f32).astype(bf16)
    rank = jnp.zeros((lines, LANES), f32)
    for t in range(TABLES):
        named = (target == t).astype(f32)
        counts = jnp.dot(named.astype(bf16), counter, preferred_element_type=f32)
        base = jnp.dot(earlier, counts[:, LANES:].astype(bf16), preferred_element_type=f32)
        rank = rank + named * (counts[:, :LANES] + base)
    rank = rank.astype(i32)
    rank_ref[...] = rank
    slot_ref[...] = target * CAP + rank
    owner = iota((TABLES, BATCH), 0)
    sample = iota((TABLES, BATCH), 1)
    spot = iota((CAP, BATCH), 0)

    def line(ref, f):
        return jnp.concatenate([ref[pl.ds(f * chunks + c, 1), :] for c in range(chunks)], axis=1)

    def feature(f, total):
        named = line(target_ref, f) == owner
        first = jnp.where(named, f + 1 + 32 * (sample // 256), 0)
        second = jnp.where(named, jnp.broadcast_to(offset_ref[pl.ds(f, 1), :], named.shape), 0)
        third = jnp.where(named, sample % 256, 0)
        values = jnp.concatenate([first, second, third], axis=0).astype(f32).astype(bf16)
        chosen = (line(rank_ref, f) == spot).astype(f32).astype(bf16)
        return total + dot_nt(values, chosen)

    total = lax.fori_loop(0, FEATS, feature, jnp.zeros((3 * TABLES, CAP), f32)).astype(i32)
    first, second, third = (total[k * TABLES : (k + 1) * TABLES] for k in range(3))
    used = first > 0
    f = first % 32 - 1
    request = jnp.where(used, f * PER_FEATURE + second, -1)
    source = jnp.where(used, f * BATCH + (first // 32) * 256 + third, 0)
    for c in range(CAP // LANES):
        request_ref[:, c, :] = request[:, c * LANES : (c + 1) * LANES]
        source_ref[:, c, :] = source[:, c * LANES : (c + 1) * LANES]


def pick(index_ref, peer, table_ref, block_ref):
    for c in range(CAP // LANES):

        def group(k, carry):
            at = pl.multiple_of(k * GROUP_OF, GROUP_OF)
            for j in range(GROUP_OF):
                row = index_ref[peer, c, at + j]
                block_ref[pl.ds(c * LANES + at + j, 1), :] = table_ref[pl.ds(row, 1), :]
            return carry

        lax.fori_loop(0, LANES // GROUP_OF, group, 0)


def trade(me, first, last, index_ref, table_ref, block_ref, rows_ref, back_ref, sent, got):
    def serve(d, carry):
        peer, _ = route(me, d)
        pick(index_ref, peer, table_ref, block_ref)
        rows_ref[peer] = block_ref[...].astype(bf16)
        push("table", peer, rows_ref.at[peer], back_ref.at[me], sent.at[d], got.at[d]).start()
        return carry

    lax.fori_loop(first, last, serve, 0)
    if last == TABLES:
        pick(index_ref, me, table_ref, block_ref)
        back_ref[me] = block_ref[...].astype(bf16)


def route(me, k):
    z, q = me // NEAR, lax.rem(me, NEAR)
    turn, step = lax.rem(k, PLANES), k // PLANES
    by = (turn + 1) // 2 * (2 * lax.rem(turn, 2) - 1)
    peer = lax.rem(z + by + PLANES, PLANES) * NEAR + lax.rem(q + step, NEAR)
    giver = lax.rem(z - by + PLANES, PLANES) * NEAR + lax.rem(q - step + NEAR, NEAR)
    return peer, giver


def finish(me, rows_ref, back_ref, sent, got):
    def settle(d, carry):
        peer, giver = route(me, d)
        push("table", peer, rows_ref.at[peer], back_ref.at[giver], sent.at[d], got.at[d]).wait()
        return carry

    lax.fori_loop(1, TABLES, settle, 0)


def fetch_kernel(
    target_ref, offset_ref, table_ref, slot_ref, source_ref, segment_ref, count_ref, back_ref,
    rank_ref, request_ref, wanted_ref, clip_ref, index_ref, block_ref, rows_ref, copied, sent_ask, got_ask, sent, got,
):
    me = lax.axis_index("table")
    hail("table", TABLES)
    place(target_ref, offset_ref, slot_ref, source_ref, request_ref, rank_ref)
    gather_in(TABLES)

    def ask(d, carry):
        peer, _ = route(me, d)
        push("table", peer, request_ref.at[peer], wanted_ref.at[me], sent_ask.at[d], got_ask.at[d]).start()
        return carry

    lax.fori_loop(1, TABLES, ask, 0)
    wanted_ref[me] = request_ref[me]
    finish(me, request_ref, wanted_ref, sent_ask, got_ask)
    wanted = wanted_ref[...]
    clip_ref[...] = jnp.clip(wanted, 0, ROWS - 1)
    copy = pltpu.make_async_copy(clip_ref, index_ref, copied)
    copy.start()
    segment_ref[...] = jnp.where(wanted >= 0, wanted, ROWS)
    used = jnp.sum((wanted >= 0).astype(f32), axis=1)
    count_ref[...] = jnp.broadcast_to(jnp.sum(used, axis=1, keepdims=True), (TABLES, LANES)).astype(i32)
    copy.wait()
    trade(me, 1, TABLES, index_ref, table_ref, block_ref, rows_ref, back_ref, sent, got)
    finish(me, rows_ref, back_ref, sent, got)


def fetch(target, offset, table):
    lists = (TABLES, CAP // LANES, LANES)
    return pl.pallas_call(
        fetch_kernel,
        out_shape=(
            jax.ShapeDtypeStruct((FEATS * BATCH // LANES, LANES), i32),
            jax.ShapeDtypeStruct(lists, i32),
            jax.ShapeDtypeStruct(lists, i32),
            jax.ShapeDtypeStruct((TABLES, LANES), i32),
            jax.ShapeDtypeStruct((TABLES, CAP, WIDTH), bf16),
        ),
        in_specs=[vmem()] * 3,
        out_specs=(vmem(),) * 5,
        scratch_shapes=[
            pltpu.VMEM((FEATS * BATCH // LANES, LANES), i32),
            pltpu.VMEM(lists, i32),
            pltpu.VMEM(lists, i32),
            pltpu.VMEM(lists, i32),
            pltpu.SMEM(lists, i32),
            pltpu.VMEM((CAP, WIDTH), f32),
            pltpu.VMEM((TABLES, CAP, WIDTH), bf16),
            pltpu.SemaphoreType.DMA,
            dma(TABLES),
            dma(TABLES),
            dma(TABLES),
            dma(TABLES),
        ],
        compiler_params=params(2),
        name="fetch",
    )(target, offset, table)


def mix_kernel(
    slot_ref, back_ref, weight_ref, label_ref, last_ref, pooled_ref, slope_ref,
    table_ref, block_ref, sum_ref, arrived_ref, sent, got, sent_slope, got_slope,
):
    me = lax.axis_index("group")
    hail("group", GROUPS)

    def widen(t, carry):
        table_ref[pl.ds(pl.multiple_of(t * CAP, CAP), CAP), :] = back_ref[t].astype(f32)
        return carry

    lax.fori_loop(0, TABLES, widen, 0)
    gather_in(GROUPS)

    def part(ref, index):
        return ref.at[pl.ds(pl.multiple_of(index * SHARE, SHARE), SHARE)]

    def pair(k, carry):
        first = lax.rem(me // 2 + 1 + k, GROUPS // 2) * 2
        base = pl.multiple_of(first * SHARE, 2 * SHARE)

        def group(b, inner):
            at = pl.multiple_of(b * 8, 8)
            for j in range(8):
                for f in range(FEATS):
                    row = slot_ref[f * BATCH + base + at + j]
                    block_ref[f, pl.ds(at + j, 1), :] = table_ref[pl.ds(row, 1), :]
            return inner

        lax.fori_loop(0, 2 * SHARE // 8, group, 0)
        pooled = jnp.concatenate([block_ref[f].astype(bf16) for f in range(FEATS)], axis=1)
        both = pl.ds(base, 2 * SHARE)
        pooled_ref[both, :] = pooled
        sum_ref[both, :] = jnp.dot(pooled, weight_ref[...], preferred_element_type=f32)
        for e in range(2):
            peer = first + e
            d = lax.rem(peer + GROUPS - me, GROUPS)

            @pl.when(d > 0)
            def _():
                push("group", peer, part(sum_ref, peer), arrived_ref.at[d], sent.at[d], got.at[d]).start()

        return carry

    lax.fori_loop(0, GROUPS // 2, pair, 0)
    mine = pl.ds(pl.multiple_of(me * SHARE, SHARE), SHARE)
    pre_act = sum_ref[mine, :]
    for d in range(1, GROUPS):
        peer = lax.rem(me + d, GROUPS)
        push("group", peer, part(sum_ref, peer), arrived_ref.at[d], sent.at[d], got.at[d]).wait()
        pre_act = pre_act + arrived_ref[d]
    sig_pre = jax.nn.sigmoid(pre_act)
    last = last_ref[...]
    logits = jnp.sum(pre_act * sig_pre * last, axis=1, keepdims=True)
    own = iota((SHARE, LANES), 1) == iota((SHARE, LANES), 0) + lax.rem(me, 2) * SHARE
    labels = label_ref[pl.ds(me // 2, 1), :].astype(f32)
    residual = jax.nn.sigmoid(logits) - jnp.sum(jnp.where(own, labels, 0.0), axis=1, keepdims=True)
    slope_ref[mine, :] = (residual * last * (sig_pre * (1.0 + pre_act * (1.0 - sig_pre)))).astype(bf16)
    for d in range(1, GROUPS):
        peer = lax.rem(me + d, GROUPS)
        push("group", peer, part(slope_ref, me), part(slope_ref, me), sent_slope.at[d], got_slope.at[d]).start()
    for d in range(1, GROUPS):
        peer = lax.rem(me + d, GROUPS)
        giver = lax.rem(me + GROUPS - d, GROUPS)
        push("group", peer, part(slope_ref, me), part(slope_ref, giver), sent_slope.at[d], got_slope.at[d]).wait()


def mix(slot, back, weight, label, last):
    return pl.pallas_call(
        mix_kernel,
        out_shape=(
            jax.ShapeDtypeStruct((BATCH, FEATS * WIDTH), bf16),
            jax.ShapeDtypeStruct((BATCH, HIDDEN), bf16),
        ),
        in_specs=[smem()] + [vmem()] * 4,
        out_specs=(vmem(), vmem()),
        scratch_shapes=[
            pltpu.VMEM((TABLES * CAP, WIDTH), f32),
            pltpu.VMEM((FEATS, 2 * SHARE, WIDTH), f32),
            pltpu.VMEM((BATCH, HIDDEN), f32),
            pltpu.VMEM((GROUPS, SHARE, HIDDEN), f32),
            dma(GROUPS),
            dma(GROUPS),
            dma(GROUPS),
            dma(GROUPS),
        ],
        compiler_params=params(0),
        name="mix",
    )(slot, back, weight, label, last)


def pack(total):
    top = jnp.max(jnp.abs(total), axis=1, keepdims=True)
    power = jnp.ceil(jnp.log2(jnp.clip(top * 1.0001, 1e-30, 1e30))) - 15.0
    scaled = jnp.floor(total * jnp.exp2(-power) + 0.5).astype(i32)
    power = jnp.broadcast_to(power.astype(i32), (OUT_ROWS, LANES))
    return jnp.concatenate([scaled, power], axis=1).astype(jnp.int16)


def unpack(packed):
    wide = packed.astype(i32).astype(f32)
    unit = jnp.exp2(wide[:, FEATS * WIDTH :])
    return wide[:, : FEATS * WIDTH] * jnp.concatenate([unit] * (FEATS * WIDTH // LANES), axis=1)


def give_kernel(
    source_ref, slope_ref, pooled_ref, weight_ref, back_ref, packed_ref,
    table_ref, block_ref, rows_ref, grad_ref, near_ref, coded_ref, across_ref, sent, got, sent_near, got_near, sent_across, got_across,
):
    me = lax.axis_index("table")
    core, side = lax.rem(me, 2), lax.rem(me // 2, 2)
    other, across = me + 1 - 2 * core, me + 2 - 4 * side
    hail("table", TABLES)

    def pair(k, carry):
        at = pl.multiple_of(k * 2 * WIDTH, 2 * WIDTH)
        both = dot_nt(slope_ref[...], weight_ref[pl.ds(at, 2 * WIDTH), :]).astype(bf16).astype(f32)
        to = pl.multiple_of(k * 2 * BATCH, 2 * BATCH)
        table_ref[pl.ds(to, BATCH), :] = both[:, :WIDTH]
        table_ref[pl.ds(to + BATCH, BATCH), :] = both[:, WIDTH:]
        return carry

    lax.fori_loop(0, FEATS // 2, pair, 0)
    gather_in(TABLES)
    trade(me, 1, EARLY, source_ref, table_ref, block_ref, rows_ref, back_ref, sent, got)

    def to_near(z):
        return push("table", other, grad_ref.at[z, :, 1 - core], near_ref.at[z], sent_near.at[z], got_near.at[z])

    def to_across(z):
        return push("table", across, coded_ref.at[z], across_ref.at[z], sent_across.at[z], got_across.at[z])

    def outer(z, carry):
        at = pl.multiple_of(z * LANES, LANES)
        part = lax.dot_general(
            slope_ref[:, pl.ds(at, LANES)], pooled_ref[...], (((0,), (0,)), ((), ())), preferred_element_type=f32
        )
        grad_ref[z] = part.reshape(grad_ref.shape[1:])
        to_near(z).start()
        return carry

    lax.fori_loop(0, PLANES, outer, 0)
    trade(me, EARLY, TABLES, source_ref, table_ref, block_ref, rows_ref, back_ref, sent, got)

    def fold(z, carry):
        to_near(z).wait()
        for x in range(2):
            grad_ref[z, x, core] = grad_ref[z, x, core] + near_ref[z, x]
        coded_ref[z] = pack(grad_ref[z, 1 - side, core])
        to_across(z).start()
        return carry

    lax.fori_loop(0, PLANES, fold, 0)

    def seal(z, carry):
        to_across(z).wait()
        total = grad_ref[z, side, core] + unpack(across_ref[z])
        packed_ref[lax.rem(z - me // NEAR + PLANES, PLANES)] = pack(total)
        return carry

    lax.fori_loop(0, PLANES, seal, 0)
    finish(me, rows_ref, back_ref, sent, got)


def give(source, slope, pooled, weight):
    piece = (OUT_ROWS, FEATS * WIDTH)
    coded = (PLANES, OUT_ROWS, FEATS * WIDTH + LANES)
    return pl.pallas_call(
        give_kernel,
        out_shape=(
            jax.ShapeDtypeStruct((TABLES, CAP, WIDTH), bf16),
            jax.ShapeDtypeStruct(coded, jnp.int16),
        ),
        in_specs=[smem(), vmem(), vmem(), vmem()],
        out_specs=(vmem(), vmem()),
        scratch_shapes=[
            pltpu.VMEM((FEATS * BATCH, WIDTH), f32),
            pltpu.VMEM((CAP, WIDTH), f32),
            pltpu.VMEM((TABLES, CAP, WIDTH), bf16),
            pltpu.VMEM((PLANES, 2, 2) + piece, f32),
            pltpu.VMEM((PLANES, 2) + piece, f32),
            pltpu.VMEM(coded, jnp.int16),
            pltpu.VMEM(coded, jnp.int16),
            dma(TABLES),
            dma(TABLES),
            dma(PLANES),
            dma(PLANES),
            dma(PLANES),
            dma(PLANES),
        ],
        compiler_params=params(3),
        name="give",
    )(source, slope, pooled, weight)


def update_kernel(
    index_ref, count_ref, slot_ref, incoming_ref, table_ref, state_ref, rows_ref, new_state_ref, stripes_ref, block_ref, *accs
):
    def clear(k, carry):
        at = pl.ds(pl.multiple_of(k * 128, 128), 128)
        for acc in accs:
            acc[at, :] = jnp.zeros((128, WIDTH), f32)
        return carry

    lax.fori_loop(0, ROWS // 128, clear, 0)

    def peer(t, carry):
        block_ref[...] = incoming_ref[t].astype(f32)

        def group(k, inner):
            at = pl.multiple_of(k * ACCS, ACCS)
            for j in range(ACCS):
                row = index_ref[t * CAP + at + j]
                accs[j][pl.ds(row, 1), :] = accs[j][pl.ds(row, 1), :] + block_ref[pl.ds(at + j, 1), :]
            return inner

        return lax.fori_loop(0, (count_ref[t, 0] + ACCS - 1) // ACCS, group, carry)

    lax.fori_loop(0, TABLES, peer, 0)
    half = WIDTH // 2
    same = iota((WIDTH, WIDTH), 0) == iota((WIDTH, WIDTH), 1)

    def stripe(s, carry):
        at = pl.ds(pl.multiple_of(s * 128, 128), 128)
        grad = accs[0][at, :]
        for acc in accs[1:]:
            grad = grad + acc[at, :]
        mean = jnp.sum(grad * grad, axis=1, keepdims=True) * (1.0 / WIDTH)
        state = jnp.sum(jnp.where(same, state_ref[pl.ds(s, 1), :], 0.0), axis=1, keepdims=True) + mean
        change = -LEARN_RATE * grad * lax.rsqrt(state)
        rows_ref[at, :] = table_ref[at, :] + change
        new_state_ref[pl.ds(s, 1), :] = jnp.sum(jnp.where(same, state, 0.0), axis=0, keepdims=True)
        stripes_ref[slot_ref[s]] = (change[:half] + change[half:]).astype(bf16)
        return carry

    lax.fori_loop(0, ROWS // 128, stripe, 0)


def update(index, count, slot, incoming, table, state):
    return pl.pallas_call(
        update_kernel,
        out_shape=(
            jax.ShapeDtypeStruct((ROWS, WIDTH), f32),
            jax.ShapeDtypeStruct((ROWS // WIDTH, WIDTH), f32),
            jax.ShapeDtypeStruct((ROWS // WIDTH, WIDTH // 2, WIDTH), bf16),
        ),
        in_specs=[smem(), smem(), smem(), vmem(), vmem(), vmem()],
        out_specs=(vmem(),) * 3,
        scratch_shapes=[pltpu.VMEM((CAP, WIDTH), f32)] + [pltpu.VMEM((ROWS + 8, WIDTH), f32)] * ACCS,
        compiler_params=params(),
        name="update",
    )(index, count, slot, incoming, table, state)


def close_kernel(
    stripes_ref, parity_ref, packed_ref, out_ref, grad_ref, arrived_ref, landed_ref, sent, got, sent_grad, got_grad
):
    me = lax.axis_index("group")
    spot = lax.axis_index("table")
    plane, q = spot // NEAR, lax.rem(spot, NEAR)

    def along(k):
        return lax.rem(plane + k, PLANES) * NEAR + q

    hail("group", GROUPS)
    barrier = pltpu.get_barrier_semaphore()
    for k in range(1, PLANES):
        pl.semaphore_signal(barrier, inc=1, device_id={"table": along(k)}, device_id_type=MESH)
    pl.semaphore_wait(barrier, GROUPS + PLANES - 2)
    shares, copies = [], []
    for k in sorted(range(1, PLANES), key=lambda k: min(k, PLANES - k)):
        shares.append(push("table", along(k), packed_ref.at[k], landed_ref.at[k], sent_grad.at[k], got_grad.at[k]))
        shares[-1].start()
    for d in range(1, GROUPS):
        peer = lax.rem(me + d, GROUPS)
        theirs = stripes_ref.at[pl.ds(peer * OWNED, OWNED)]
        copies.append(push("group", peer, theirs, arrived_ref.at[d], sent.at[d], got.at[d]))
        copies[-1].start()
    total = stripes_ref[pl.ds(me * OWNED, OWNED)].astype(f32)
    grad_ref[...] = unpack(packed_ref[0])
    for copy in copies:
        copy.wait()
    for d in range(1, GROUPS):
        total = total + arrived_ref[d].astype(f32)
    out_ref[...] = parity_ref[...] + total
    for copy in shares:
        copy.wait()
    for k in range(1, PLANES):
        grad_ref[...] = grad_ref[...] + unpack(landed_ref[k])


def close(stripes, parity, packed):
    return pl.pallas_call(
        close_kernel,
        out_shape=(
            jax.ShapeDtypeStruct(parity.shape, f32),
            jax.ShapeDtypeStruct((OUT_ROWS, FEATS * WIDTH), f32),
        ),
        in_specs=[vmem()] * 3,
        out_specs=(vmem(), vmem()),
        scratch_shapes=[
            pltpu.VMEM((GROUPS,) + parity.shape, bf16),
            pltpu.VMEM(packed.shape, jnp.int16),
            dma(GROUPS),
            dma(GROUPS),
            dma(PLANES),
            dma(PLANES),
        ],
        compiler_params=params(1),
        name="close",
    )(stripes, parity, packed)


def local(
    table_rows,
    row_state,
    parity,
    parity_slot,
    row_shard,
    row_offset,
    labels,
    first_weight,
    last_weight,
):
    table = table_rows[0]
    target = jnp.transpose(row_shard.reshape(BATCH // LANES, LANES, FEATS), (2, 0, 1)).reshape(-1, LANES)
    offset = jnp.transpose(row_offset[0])
    slot, source, segment, served, back = fetch(target, offset, table)
    pooled, slope = mix(slot.reshape(-1), back, first_weight, labels.reshape(-1, LANES), last_weight[None, :])
    incoming, packed = give(source, slope, pooled, first_weight)
    new_rows, new_state, stripes = update(
        segment.reshape(-1), served, parity_slot[0], incoming, table, row_state.reshape(ROWS // WIDTH, WIDTH)
    )
    new_parity, first_grad = close(stripes, parity[0], packed)
    return (new_rows[None], new_state.reshape(1, ROWS), new_parity[None], first_grad)


def solution(mesh):
    placed = (
        P("group", "table", None),
        P("group", "table"),
        P("table", "group", None, None),
        P("table", None),
        P("group", "table", None, None),
        P("group", "table", None),
        P("table"),
        P("group", None),
        P(),
    )
    return jax.shard_map(
        local,
        mesh=mesh,
        in_specs=placed,
        out_specs=(
            P("group", "table", None),
            P("group", "table"),
            P("table", "group", None, None),
            P("table", "group"),
        ),
        check_vma=False,
    )
```

```python
import functools

import jax
import jax.numpy as jnp
from jax import lax
from jax.experimental import pallas as pl
from jax.experimental.pallas import tpu as pltpu
from jax.sharding import PartitionSpec as P

LEARN_RATE = 0.1
GROUPS = 8
TABLES = 32
CAP = 512
FEATS = 16
BATCH = 512
ROWS = 4096
PER_FEATURE = 256
WIDTH = 128
HIDDEN = 1024
NEAR = 4
PLANES = TABLES // NEAR
OUT_ROWS = HIDDEN // TABLES
EARLY = 5
MIDWAY = 17
SHARE = BATCH // GROUPS
OWNED = 32 // GROUPS
LANES = 128
GROUP_OF = 16
ACCS = 8
VMEM_BYTES = 56 * 2**20

f32 = jnp.float32
bf16 = jnp.bfloat16
i32 = jnp.int32
MESH = pl.DeviceIdType.MESH


def params(collective_id=None):
    if collective_id is None:
        return pltpu.CompilerParams(vmem_limit_bytes=VMEM_BYTES)
    return pltpu.CompilerParams(vmem_limit_bytes=VMEM_BYTES, collective_id=collective_id, has_side_effects=True)


def vmem():
    return pl.BlockSpec(memory_space=pltpu.VMEM)


def smem():
    return pl.BlockSpec(memory_space=pltpu.SMEM)


def dot_nt(a, b):
    return lax.dot_general(a, b, (((1,), (1,)), ((), ())), preferred_element_type=f32)


def iota(shape, axis):
    return lax.broadcasted_iota(i32, shape, axis)


def hail(axis, size):
    me = lax.axis_index(axis)
    barrier = pltpu.get_barrier_semaphore()
    for d in range(1, size):
        pl.semaphore_signal(barrier, inc=1, device_id={axis: lax.rem(me + d, size)}, device_id_type=MESH)


def gather_in(size):
    pl.semaphore_wait(pltpu.get_barrier_semaphore(), size - 1)


def push(axis, peer, source, target, sent, got):
    return pltpu.make_async_remote_copy(
        src_ref=source, dst_ref=target, send_sem=sent, recv_sem=got, device_id={axis: peer}, device_id_type=MESH
    )


def dma(count):
    return pltpu.SemaphoreType.DMA((count,))


def place(target_ref, offset_ref, slot_ref, source_ref, request_ref, rank_ref):
    chunks = BATCH // LANES
    lines = chunks * FEATS
    target = target_ref[...]
    row, col = iota((LANES, LANES), 0), iota((LANES, LANES), 1)
    before = (row < col).astype(f32).astype(bf16)
    counter = jnp.concatenate([before, jnp.ones((LANES, LANES), bf16)], axis=1)
    earlier = (iota((lines, lines), 1) < iota((lines, lines), 0)).astype(f32).astype(bf16)
    rank = jnp.zeros((lines, LANES), f32)
    for t in range(TABLES):
        named = (target == t).astype(f32)
        counts = jnp.dot(named.astype(bf16), counter, preferred_element_type=f32)
        base = jnp.dot(earlier, counts[:, LANES:].astype(bf16), preferred_element_type=f32)
        rank = rank + named * (counts[:, :LANES] + base)
    rank = rank.astype(i32)
    rank_ref[...] = rank
    slot_ref[...] = target * CAP + rank
    owner = iota((TABLES, BATCH), 0)
    sample = iota((TABLES, BATCH), 1)
    spot = iota((CAP, BATCH), 0)

    def line(ref, f):
        return jnp.concatenate([ref[pl.ds(f * chunks + c, 1), :] for c in range(chunks)], axis=1)

    def feature(f, total):
        named = line(target_ref, f) == owner
        first = jnp.where(named, f + 1 + 32 * (sample // 256), 0)
        second = jnp.where(named, jnp.broadcast_to(offset_ref[pl.ds(f, 1), :], named.shape), 0)
        third = jnp.where(named, sample % 256, 0)
        values = jnp.concatenate([first, second, third, third], axis=0).astype(f32).astype(bf16)
        chosen = (line(rank_ref, f) == spot).astype(f32).astype(bf16)
        return total + dot_nt(chosen, values)

    total = lax.fori_loop(0, FEATS, feature, jnp.zeros((CAP, 4 * TABLES), f32)).T.astype(i32)
    first, second, third = (total[k * TABLES : (k + 1) * TABLES] for k in range(3))
    used = first > 0
    f = first % 32 - 1
    request = jnp.where(used, f * PER_FEATURE + second, -1)
    source = jnp.where(used, f * BATCH + (first // 32) * 256 + third, 0)
    for c in range(CAP // LANES):
        request_ref[:, c, :] = request[:, c * LANES : (c + 1) * LANES]
        source_ref[:, c, :] = source[:, c * LANES : (c + 1) * LANES]


def pick(index_ref, peer, table_ref, block_ref):
    for c in range(CAP // LANES):

        def group(k, carry):
            at = pl.multiple_of(k * GROUP_OF, GROUP_OF)
            for j in range(GROUP_OF):
                row = index_ref[peer, c, at + j]
                block_ref[pl.ds(c * LANES + at + j, 1), :] = table_ref[pl.ds(row, 1), :]
            return carry

        lax.fori_loop(0, LANES // GROUP_OF, group, 0)


def trade(me, first, last, index_ref, table_ref, block_ref, rows_ref, back_ref, sent, got):
    def serve(d, carry):
        peer, _ = route(me, d)
        pick(index_ref, peer, table_ref, block_ref)
        rows_ref[peer] = block_ref[...].astype(bf16)
        push("table", peer, rows_ref.at[peer], back_ref.at[me], sent.at[d], got.at[d]).start()
        return carry

    lax.fori_loop(first, last, serve, 0)
    if last == TABLES:
        pick(index_ref, me, table_ref, block_ref)
        back_ref[me] = block_ref[...].astype(bf16)


def route(me, k):
    z, q = me // NEAR, lax.rem(me, NEAR)
    turn, step = lax.rem(k, PLANES), k // PLANES
    by = (turn + 1) // 2 * (2 * lax.rem(turn, 2) - 1)
    peer = lax.rem(z + by + PLANES, PLANES) * NEAR + lax.rem(q + step, NEAR)
    giver = lax.rem(z - by + PLANES, PLANES) * NEAR + lax.rem(q - step + NEAR, NEAR)
    return peer, giver


def finish(me, rows_ref, back_ref, sent, got):
    def settle(d, carry):
        peer, giver = route(me, d)
        push("table", peer, rows_ref.at[peer], back_ref.at[giver], sent.at[d], got.at[d]).wait()
        return carry

    lax.fori_loop(1, TABLES, settle, 0)


def fetch_kernel(
    target_ref, offset_ref, table_ref, slot_ref, source_ref, segment_ref, count_ref, back_ref,
    rank_ref, request_ref, wanted_ref, clip_ref, index_ref, block_ref, rows_ref, copied, sent_ask, got_ask, sent, got,
):
    me = lax.axis_index("table")
    hail("table", TABLES)
    place(target_ref, offset_ref, slot_ref, source_ref, request_ref, rank_ref)
    gather_in(TABLES)

    def ask(d, carry):
        peer, _ = route(me, d)
        push("table", peer, request_ref.at[peer], wanted_ref.at[me], sent_ask.at[d], got_ask.at[d]).start()
        return carry

    lax.fori_loop(1, TABLES, ask, 0)
    wanted_ref[me] = request_ref[me]
    finish(me, request_ref, wanted_ref, sent_ask, got_ask)
    wanted = wanted_ref[...]
    clip_ref[...] = jnp.clip(wanted, 0, ROWS - 1)
    copy = pltpu.make_async_copy(clip_ref, index_ref, copied)
    copy.start()
    segment_ref[...] = jnp.where(wanted >= 0, wanted, ROWS)
    used = jnp.sum((wanted >= 0).astype(f32), axis=1)
    count_ref[...] = jnp.broadcast_to(jnp.sum(used, axis=1, keepdims=True), (TABLES, LANES)).astype(i32)
    copy.wait()
    trade(me, 1, TABLES, index_ref, table_ref, block_ref, rows_ref, back_ref, sent, got)
    finish(me, rows_ref, back_ref, sent, got)


def fetch(target, offset, table):
    lists = (TABLES, CAP // LANES, LANES)
    return pl.pallas_call(
        fetch_kernel,
        out_shape=(
            jax.ShapeDtypeStruct((FEATS * BATCH // LANES, LANES), i32),
            jax.ShapeDtypeStruct(lists, i32),
            jax.ShapeDtypeStruct(lists, i32),
            jax.ShapeDtypeStruct((TABLES, LANES), i32),
            jax.ShapeDtypeStruct((TABLES, CAP, WIDTH), bf16),
        ),
        in_specs=[vmem()] * 3,
        out_specs=(vmem(),) * 5,
        scratch_shapes=[
            pltpu.VMEM((FEATS * BATCH // LANES, LANES), i32),
            pltpu.VMEM(lists, i32),
            pltpu.VMEM(lists, i32),
            pltpu.VMEM(lists, i32),
            pltpu.SMEM(lists, i32),
            pltpu.VMEM((CAP, WIDTH), f32),
            pltpu.VMEM((TABLES, CAP, WIDTH), bf16),
            pltpu.SemaphoreType.DMA,
            dma(TABLES),
            dma(TABLES),
            dma(TABLES),
            dma(TABLES),
        ],
        compiler_params=params(2),
        name="fetch",
    )(target, offset, table)


def mix_kernel(
    slot_ref, back_ref, weight_ref, label_ref, last_ref, pooled_ref, slope_ref,
    table_ref, block_ref, sum_ref, arrived_ref, sent, got, sent_slope, got_slope,
):
    me = lax.axis_index("group")
    hail("group", GROUPS)

    def widen(t, carry):
        table_ref[pl.ds(pl.multiple_of(t * CAP, CAP), CAP), :] = back_ref[t].astype(f32)
        return carry

    lax.fori_loop(0, TABLES, widen, 0)
    gather_in(GROUPS)

    def part(ref, index):
        return ref.at[pl.ds(pl.multiple_of(index * SHARE, SHARE), SHARE)]

    def pair(k, carry):
        first = lax.rem(me // 2 + 1 + k, GROUPS // 2) * 2
        base = pl.multiple_of(first * SHARE, 2 * SHARE)

        def group(b, inner):
            at = pl.multiple_of(b * 8, 8)
            for j in range(8):
                for f in range(FEATS):
                    row = slot_ref[f * BATCH + base + at + j]
                    block_ref[f, pl.ds(at + j, 1), :] = table_ref[pl.ds(row, 1), :]
            return inner

        lax.fori_loop(0, 2 * SHARE // 8, group, 0)
        pooled = jnp.concatenate([block_ref[f].astype(bf16) for f in range(FEATS)], axis=1)
        both = pl.ds(base, 2 * SHARE)
        pooled_ref[both, :] = pooled
        sum_ref[both, :] = jnp.dot(pooled, weight_ref[...], preferred_element_type=f32)
        for e in range(2):
            peer = first + e
            d = lax.rem(peer + GROUPS - me, GROUPS)

            @pl.when(d > 0)
            def _():
                push("group", peer, part(sum_ref, peer), arrived_ref.at[d], sent.at[d], got.at[d]).start()

        return carry

    lax.fori_loop(0, GROUPS // 2, pair, 0)
    mine = pl.ds(pl.multiple_of(me * SHARE, SHARE), SHARE)
    pre_act = sum_ref[mine, :]
    for d in range(1, GROUPS):
        peer = lax.rem(me + d, GROUPS)
        push("group", peer, part(sum_ref, peer), arrived_ref.at[d], sent.at[d], got.at[d]).wait()
        pre_act = pre_act + arrived_ref[d]
    sig_pre = jax.nn.sigmoid(pre_act)
    last = last_ref[...]
    logits = jnp.sum(pre_act * sig_pre * last, axis=1, keepdims=True)
    own = iota((SHARE, LANES), 1) == iota((SHARE, LANES), 0) + lax.rem(me, 2) * SHARE
    labels = label_ref[pl.ds(me // 2, 1), :].astype(f32)
    residual = jax.nn.sigmoid(logits) - jnp.sum(jnp.where(own, labels, 0.0), axis=1, keepdims=True)
    slope_ref[mine, :] = (residual * last * (sig_pre * (1.0 + pre_act * (1.0 - sig_pre)))).astype(bf16)
    for d in range(1, GROUPS):
        peer = lax.rem(me + d, GROUPS)
        push("group", peer, part(slope_ref, me), part(slope_ref, me), sent_slope.at[d], got_slope.at[d]).start()
    for d in range(1, GROUPS):
        peer = lax.rem(me + d, GROUPS)
        giver = lax.rem(me + GROUPS - d, GROUPS)
        push("group", peer, part(slope_ref, me), part(slope_ref, giver), sent_slope.at[d], got_slope.at[d]).wait()


def mix(slot, back, weight, label, last):
    return pl.pallas_call(
        mix_kernel,
        out_shape=(
            jax.ShapeDtypeStruct((BATCH, FEATS * WIDTH), bf16),
            jax.ShapeDtypeStruct((BATCH, HIDDEN), bf16),
        ),
        in_specs=[smem()] + [vmem()] * 4,
        out_specs=(vmem(), vmem()),
        scratch_shapes=[
            pltpu.VMEM((TABLES * CAP, WIDTH), f32),
            pltpu.VMEM((FEATS, 2 * SHARE, WIDTH), f32),
            pltpu.VMEM((BATCH, HIDDEN), f32),
            pltpu.VMEM((GROUPS, SHARE, HIDDEN), f32),
            dma(GROUPS),
            dma(GROUPS),
            dma(GROUPS),
            dma(GROUPS),
        ],
        compiler_params=params(0),
        name="mix",
    )(slot, back, weight, label, last)


def pack(total):
    top = jnp.max(jnp.abs(total), axis=1, keepdims=True)
    power = jnp.ceil(jnp.log2(jnp.clip(top * 1.0001, 1e-30, 1e30))) - 15.0
    scaled = jnp.floor(total * jnp.exp2(-power) + 0.5).astype(i32)
    power = jnp.broadcast_to(power.astype(i32), (OUT_ROWS, LANES))
    return jnp.concatenate([scaled, power], axis=1).astype(jnp.int16)


def unpack(packed):
    wide = packed.astype(i32).astype(f32)
    unit = jnp.exp2(wide[:, FEATS * WIDTH :])
    return wide[:, : FEATS * WIDTH] * jnp.concatenate([unit] * (FEATS * WIDTH // LANES), axis=1)


def give_kernel(
    source_ref, slope_ref, pooled_ref, weight_ref, back_ref, total_ref,
    table_ref, block_ref, rows_ref, grad_ref, near_ref, coded_ref, across_ref, packed_ref, landed_ref,
    sent, got, sent_near, got_near, sent_across, got_across, sent_along, got_along,
):
    me = lax.axis_index("table")
    core, side, plane, q = lax.rem(me, 2), lax.rem(me // 2, 2), me // NEAR, lax.rem(me, NEAR)
    other, across = me + 1 - 2 * core, me + 2 - 4 * side
    hail("table", TABLES)

    def pair(k, carry):
        at = pl.multiple_of(k * 2 * WIDTH, 2 * WIDTH)
        both = dot_nt(slope_ref[...], weight_ref[pl.ds(at, 2 * WIDTH), :]).astype(bf16).astype(f32)
        to = pl.multiple_of(k * 2 * BATCH, 2 * BATCH)
        table_ref[pl.ds(to, BATCH), :] = both[:, :WIDTH]
        table_ref[pl.ds(to + BATCH, BATCH), :] = both[:, WIDTH:]
        return carry

    lax.fori_loop(0, FEATS // 2, pair, 0)
    gather_in(TABLES)
    trade(me, 1, EARLY, source_ref, table_ref, block_ref, rows_ref, back_ref, sent, got)

    def to_near(z):
        return push("table", other, grad_ref.at[z, :, 1 - core], near_ref.at[z], sent_near.at[z], got_near.at[z])

    def to_across(z):
        return push("table", across, coded_ref.at[z], across_ref.at[z], sent_across.at[z], got_across.at[z])

    def to_along(k):
        peer = lax.rem(plane + k, PLANES) * NEAR + q
        return push("table", peer, packed_ref.at[k], landed_ref.at[k], sent_along.at[k], got_along.at[k])

    def ahead(turn):
        by = (PLANES - turn) // 2 * (1 - 2 * lax.rem(turn, 2))
        return lax.rem(by + PLANES, PLANES)

    def outer(turn, carry):
        z = lax.rem(plane + ahead(turn), PLANES)
        at = pl.multiple_of(z * LANES, LANES)
        part = lax.dot_general(
            slope_ref[:, pl.ds(at, LANES)], pooled_ref[...], (((0,), (0,)), ((), ())), preferred_element_type=f32
        )
        grad_ref[z] = part.reshape(grad_ref.shape[1:])
        to_near(z).start()
        return carry

    lax.fori_loop(0, PLANES, outer, 0)
    trade(me, EARLY, MIDWAY, source_ref, table_ref, block_ref, rows_ref, back_ref, sent, got)

    def fold(turn, carry):
        z = lax.rem(plane + ahead(turn), PLANES)
        to_near(z).wait()
        for x in range(2):
            grad_ref[z, x, core] = grad_ref[z, x, core] + near_ref[z, x]
        coded_ref[z] = pack(grad_ref[z, 1 - side, core])
        to_across(z).start()
        return carry

    lax.fori_loop(0, PLANES, fold, 0)
    trade(me, MIDWAY, TABLES, source_ref, table_ref, block_ref, rows_ref, back_ref, sent, got)

    def seal(turn, carry):
        k = ahead(turn)
        z = lax.rem(plane + k, PLANES)
        to_across(z).wait()
        packed_ref[k] = pack(grad_ref[z, side, core] + unpack(across_ref[z]))
        to_along(k).start()
        return carry

    lax.fori_loop(0, PLANES - 1, seal, 0)
    to_across(plane).wait()
    total_ref[...] = grad_ref[plane, side, core] + unpack(across_ref[plane])
    finish(me, rows_ref, back_ref, sent, got)

    def land(turn, carry):
        k = ahead(turn)
        to_along(k).wait()
        total_ref[...] = total_ref[...] + unpack(landed_ref[k])
        return carry

    lax.fori_loop(0, PLANES - 1, land, 0)


def give(source, slope, pooled, weight):
    piece = (OUT_ROWS, FEATS * WIDTH)
    coded = (PLANES, OUT_ROWS, FEATS * WIDTH + LANES)
    return pl.pallas_call(
        give_kernel,
        out_shape=(
            jax.ShapeDtypeStruct((TABLES, CAP, WIDTH), bf16),
            jax.ShapeDtypeStruct(piece, f32),
        ),
        in_specs=[smem(), vmem(), vmem(), vmem()],
        out_specs=(vmem(), vmem()),
        scratch_shapes=[
            pltpu.VMEM((FEATS * BATCH, WIDTH), f32),
            pltpu.VMEM((CAP, WIDTH), f32),
            pltpu.VMEM((TABLES, CAP, WIDTH), bf16),
            pltpu.VMEM((PLANES, 2, 2) + piece, f32),
            pltpu.VMEM((PLANES, 2) + piece, f32),
            pltpu.VMEM(coded, jnp.int16),
            pltpu.VMEM(coded, jnp.int16),
            pltpu.VMEM(coded, jnp.int16),
            pltpu.VMEM(coded, jnp.int16),
            dma(TABLES),
            dma(TABLES),
            dma(PLANES),
            dma(PLANES),
            dma(PLANES),
            dma(PLANES),
            dma(PLANES),
            dma(PLANES),
        ],
        compiler_params=params(3),
        name="give",
    )(source, slope, pooled, weight)


def update_kernel(
    index_ref, count_ref, slot_ref, incoming_ref, table_ref, state_ref, rows_ref, new_state_ref, stripes_ref, block_ref, *accs
):
    def clear(k, carry):
        at = pl.ds(pl.multiple_of(k * 128, 128), 128)
        for acc in accs:
            acc[at, :] = jnp.zeros((128, WIDTH), f32)
        return carry

    lax.fori_loop(0, ROWS // 128, clear, 0)

    def peer(t, carry):
        block_ref[...] = incoming_ref[t].astype(f32)

        def group(k, inner):
            at = pl.multiple_of(k * ACCS, ACCS)
            for j in range(ACCS):
                row = index_ref[t * CAP + at + j]
                accs[j][pl.ds(row, 1), :] = accs[j][pl.ds(row, 1), :] + block_ref[pl.ds(at + j, 1), :]
            return inner

        return lax.fori_loop(0, (count_ref[t, 0] + ACCS - 1) // ACCS, group, carry)

    lax.fori_loop(0, TABLES, peer, 0)
    half = WIDTH // 2
    same = iota((WIDTH, WIDTH), 0) == iota((WIDTH, WIDTH), 1)

    def stripe(s, carry):
        at = pl.ds(pl.multiple_of(s * 128, 128), 128)
        grad = accs[0][at, :]
        for acc in accs[1:]:
            grad = grad + acc[at, :]
        mean = jnp.sum(grad * grad, axis=1, keepdims=True) * (1.0 / WIDTH)
        state = jnp.sum(jnp.where(same, state_ref[pl.ds(s, 1), :], 0.0), axis=1, keepdims=True) + mean
        change = -LEARN_RATE * grad * lax.rsqrt(state)
        rows_ref[at, :] = table_ref[at, :] + change
        new_state_ref[pl.ds(s, 1), :] = jnp.sum(jnp.where(same, state, 0.0), axis=0, keepdims=True)
        stripes_ref[slot_ref[s]] = (change[:half] + change[half:]).astype(bf16)
        return carry

    lax.fori_loop(0, ROWS // 128, stripe, 0)


def update(index, count, slot, incoming, table, state):
    return pl.pallas_call(
        update_kernel,
        out_shape=(
            jax.ShapeDtypeStruct((ROWS, WIDTH), f32),
            jax.ShapeDtypeStruct((ROWS // WIDTH, WIDTH), f32),
            jax.ShapeDtypeStruct((ROWS // WIDTH, WIDTH // 2, WIDTH), bf16),
        ),
        in_specs=[smem(), smem(), smem(), vmem(), vmem(), vmem()],
        out_specs=(vmem(),) * 3,
        scratch_shapes=[pltpu.VMEM((CAP, WIDTH), f32)] + [pltpu.VMEM((ROWS + 8, WIDTH), f32)] * ACCS,
        compiler_params=params(),
        name="update",
    )(index, count, slot, incoming, table, state)


def stripe_kernel(stripes_ref, parity_ref, out_ref, arrived_ref, sent, got):
    me = lax.axis_index("group")
    hail("group", GROUPS)
    gather_in(GROUPS)
    copies = []
    for d in range(1, GROUPS):
        peer = lax.rem(me + d, GROUPS)
        theirs = stripes_ref.at[pl.ds(peer * OWNED, OWNED)]
        copies.append(push("group", peer, theirs, arrived_ref.at[d], sent.at[d], got.at[d]))
        copies[-1].start()
    total = stripes_ref[pl.ds(me * OWNED, OWNED)].astype(f32)
    for copy in copies:
        copy.wait_recv()
    for d in range(1, GROUPS):
        total = total + arrived_ref[d].astype(f32)
    out_ref[...] = parity_ref[...] + total
    for copy in copies:
        copy.wait_send()


def stripe_sum(stripes, parity):
    return pl.pallas_call(
        stripe_kernel,
        out_shape=jax.ShapeDtypeStruct(parity.shape, f32),
        in_specs=[vmem()] * 2,
        out_specs=vmem(),
        scratch_shapes=[pltpu.VMEM((GROUPS,) + parity.shape, bf16)] + [pltpu.SemaphoreType.DMA((GROUPS,))] * 2,
        compiler_params=params(1),
        name="stripe_sum",
    )(stripes, parity)


def local(
    table_rows,
    row_state,
    parity,
    parity_slot,
    row_shard,
    row_offset,
    labels,
    first_weight,
    last_weight,
):
    table = table_rows[0]
    target = jnp.transpose(row_shard.reshape(BATCH // LANES, LANES, FEATS), (2, 0, 1)).reshape(-1, LANES)
    offset = jnp.transpose(row_offset[0])
    slot, source, segment, served, back = fetch(target, offset, table)
    pooled, slope = mix(slot.reshape(-1), back, first_weight, labels.reshape(-1, LANES), last_weight[None, :])
    incoming, first_grad = give(source, slope, pooled, first_weight)
    new_rows, new_state, stripes = update(
        segment.reshape(-1), served, parity_slot[0], incoming, table, row_state.reshape(ROWS // WIDTH, WIDTH)
    )
    new_parity = stripe_sum(stripes, parity[0])
    return (new_rows[None], new_state.reshape(1, ROWS), new_parity[None], first_grad)


def solution(mesh):
    placed = (
        P("group", "table", None),
        P("group", "table"),
        P("table", "group", None, None),
        P("table", None),
        P("group", "table", None, None),
        P("group", "table", None),
        P("table"),
        P("group", None),
        P(),
    )
    return jax.shard_map(
        local,
        mesh=mesh,
        in_specs=placed,
        out_specs=(
            P("group", "table", None),
            P("group", "table"),
            P("table", "group", None, None),
            P("table", "group"),
        ),
        check_vma=False,
    )
```
